128 devices in a mesh: gx: 2 (over core), gy: 8 (over y_lo, x), gz: 8 (over y_hi, z).
Axes of the slice: x: 4, y: 4 (y_hi: 2, y_lo: 2; y = y_hi * 2 + y_lo), z: 4, core: 2. Of those that a mesh axis runs over, the one named last changes fastest.
Arguments:
- inputs: bfloat16 [1280, 6144], P('gx', ('gy', 'gz')), may hold values from -6 to 6
- out_grad: bfloat16 [1280, 6144], P('gx', ('gy', 'gz')), may hold values from -6 to 6
- up_weight: bfloat16 [6144, 24576], P('gy', ('gx', 'gz')), may hold values from -0.078125 to 0.078125
- down_weight: bfloat16 [24576, 6144], P(('gx', 'gz'), 'gy'), may hold values from -0.0390625 to 0.0390625
Outputs:
- in_grad: bfloat16 [1280, 6144], P('gx', ('gy', 'gz'))
- up_weight_grad: bfloat16 [6144, 24576], P('gy', ('gx', 'gz'))
- down_weight_grad: bfloat16 [24576, 6144], P(('gx', 'gz'), 'gy')
The draws below stay inside these ranges and needn't reach their ends.
All inputs are finite; a program needn't handle non-finite values.
Results may differ from the reference program's by a relative error of at most 0.005.
Values may be sent and summed in bfloat16 or wider, within the bound.
A program may use at most 128 MiB of HBM per device.

```python
import jax
import jax.numpy as jnp
from jax import lax

D = 6144
FF = 24576
TOKENS = 1280


def block_scale(stream_key, extent, pieces, least, high):
    loudness = 1.0
    for dim, blocks in pieces:
        steps = jax.random.uniform(jax.random.fold_in(jax.random.fold_in(stream_key, 6), dim), (blocks,), jnp.float32, least / len(pieces), high / len(pieces))
        loudness = loudness * jnp.repeat(jnp.exp(steps), extent[dim] // blocks).reshape((-1,) + (1,) * (len(extent) - 1 - dim))
    return loudness


def scatter_about(rng, shape, scale, bound, split=(), held_as=jnp.bfloat16):
    gain = block_scale(rng, shape, split, -0.22, 0.18) if split else 1.0
    array = jax.random.normal(rng, shape, jnp.float32) * scale * gain
    return jnp.minimum(jnp.maximum(array, -bound), bound).astype(held_as)


def setup_inputs(seed: int = 0) -> dict:
    key_list = jax.random.split(jax.random.key(seed), 5)
    inputs = scatter_about(key_list[0], (TOKENS, D), 1.0, 6.0, ((0, 2), (1, 64)))
    out_grad = scatter_about(key_list[1], (TOKENS, D), 1.0, 6.0, ((0, 2), (1, 64)))
    up_weight = scatter_about(key_list[2], (D, FF), D ** -0.5, 0.078125, ((0, 8), (1, 16)))
    down_weight = scatter_about(key_list[3], (FF, D), FF ** -0.5, 0.0390625, ((0, 16), (1, 8)))
    return {"inputs": inputs, "out_grad": out_grad, "up_weight": up_weight, "down_weight": down_weight}


gelu_scale = 0.7978845608028654
cubic_term = 0.044715


def activate(hidden_pre, act_grad):
    inner = gelu_scale * (hidden_pre + cubic_term * hidden_pre * hidden_pre * hidden_pre)
    tanh_val = jnp.tanh(inner)
    activation = 0.5 * hidden_pre * (1.0 + tanh_val)
    deriv = 0.5 * (1.0 + tanh_val) + 0.5 * hidden_pre * (1.0 - tanh_val * tanh_val) * gelu_scale * (1.0 + 3.0 * cubic_term * hidden_pre * hidden_pre)
    return activation.astype(jnp.bfloat16), (act_grad * deriv).astype(jnp.bfloat16)


def reference(inputs, out_grad, up_weight, down_weight):
    hidden_pre = jnp.dot(inputs, up_weight, preferred_element_type=jnp.float32)
    act_grad = lax.dot_general(out_grad, down_weight, (((1,), (1,)), ((), ())), preferred_element_type=jnp.float32)
    activation, pre_grad = activate(hidden_pre, act_grad)
    in_grad = lax.dot_general(pre_grad, up_weight, (((1,), (1,)), ((), ())), preferred_element_type=jnp.float32)
    up_weight_grad = lax.dot_general(inputs, pre_grad, (((0,), (0,)), ((), ())), preferred_element_type=jnp.float32)
    down_weight_grad = lax.dot_general(activation, out_grad, (((0,), (0,)), ((), ())), preferred_element_type=jnp.float32)
    return in_grad.astype(jnp.bfloat16), up_weight_grad.astype(jnp.bfloat16), down_weight_grad.astype(jnp.bfloat16)
```

```python
import functools

import jax
import jax.numpy as jnp
from jax import lax
from jax.experimental import pallas as pl
from jax.experimental.pallas import tpu as pltpu
from jax.sharding import PartitionSpec as P

gelu_scale = 0.7978845608028654
cubic_term = 0.044715

MESH = pl.DeviceIdType.MESH
BF16, F32 = jnp.bfloat16, jnp.float32

CHUNKS = ((0, 256), (256, 384))
SEMS = 90 * len(CHUNKS)


def nn(left, right):
    return jnp.dot(left, right, preferred_element_type=F32)


def nt(left, right):
    return lax.dot_general(left, right, (((1,), (1,)), ((), ())), preferred_element_type=F32)


def aligned(index, step):
    return pl.multiple_of(index * step, step)


class Place:
    def __init__(self):
        self.c = lax.axis_index("gx")
        self.gy = lax.axis_index("gy")
        self.gz = lax.axis_index("gz")
        self.yl, self.x = self.gy // 4, self.gy % 4
        self.yh, self.z = self.gz // 4, self.gz % 4

    def dev(self, dc=0, dyl=0, dx=0, dyh=0, dz=0):
        return (
            (self.c + dc) % 2,
            self.owner((self.yl + dyl) % 2, dx),
            self.zblock(dyh, dz),
        )

    def owner(self, row, dx):
        return row * 4 + (self.x + dx) % 4

    def zblock(self, dyh, dz):
        return ((self.yh + dyh) % 2) * 4 + (self.z + dz) % 4


class Net:
    def __init__(self, send_sems, recv_sems):
        self.send_sems, self.recv_sems = send_sems, recv_sems
        self.copies = []

    def send(self, src, dst, device):
        i = len(self.copies)
        assert i < SEMS
        copy = pltpu.make_async_remote_copy(
            src_ref=src,
            dst_ref=dst,
            send_sem=self.send_sems.at[i],
            recv_sem=self.recv_sems.at[i],
            device_id=device,
            device_id_type=MESH,
        )
        copy.start()
        self.copies.append(copy)
        return copy

    def drain(self):
        for copy in self.copies:
            copy.wait_send()


class Ring:
    def __init__(self, net, here, out, far, near, partial):
        self.net, self.out, self.far, self.near, self.partial = net, out, far, near, partial
        self.right, self.left = here.dev(dx=1), here.dev(dx=3)
        self.h = out.shape[1] // 2

    def half(self, i):
        return pl.ds(i * self.h, self.h)

    def push(self, slot, half, value, dst, device):
        src = self.out.at[slot, self.half(half)]
        src[...] = value.astype(BF16)
        return self.net.send(src, dst, device)

    def opposite(self):
        self.far_copies = [
            self.push(0, 0, self.partial(2, 0), self.far.at[0], self.right),
            self.push(0, 1, self.partial(2, 1), self.far.at[1], self.left),
        ]

    def beside(self):
        self.near_copies = [
            self.push(1, 1, self.partial(1, 1), self.near.at[0, self.half(1)], self.right),
            self.push(2, 0, self.partial(3, 0), self.near.at[1, self.half(0)], self.left),
        ]

    def relay(self):
        for i, (slot, dx, device) in enumerate(((1, 1, self.right), (2, 3, self.left))):
            part = self.partial(dx, i)
            self.far_copies[i].wait_recv()
            value = part + self.far[i].astype(F32)
            self.near_copies.append(
                self.push(slot, i, value, self.near.at[i, self.half(i)], device)
            )

    def arrive(self):
        for copy in self.near_copies:
            copy.wait_recv()

    def total(self, half):
        rows = self.half(half)
        return (
            self.partial(0, half)
            + self.near[0, rows].astype(F32)
            + self.near[1, rows].astype(F32)
        )


class YFirst:
    def __init__(self, net, here, bufs, weight, acts, block):
        self.net, self.here, self.bufs, self.block = net, here, bufs, block
        self.weight, self.acts = weight, acts
        self.waited = set()
        self.ring = Ring(net, here, bufs["out"].at[0], bufs["far"].at[0], bufs["near"].at[0], self.partial)

    def product(self, row, dx, half):
        h = self.block // 2
        first = aligned(self.here.owner(row, dx) * 2 + half, h)
        return nn(self.weight[pl.ds(first, h), :], self.acts[...])

    def partial(self, dx, half):
        if dx not in self.waited:
            self.y_copies[dx].wait_recv()
            self.waited.add(dx)
        h = self.block // 2
        return self.product(self.here.yl, dx, half) + self.bufs["y_in"][dx, pl.ds(half * h, h)].astype(F32)

    def start(self):
        self.y_copies = {}
        h = self.block // 2
        for dx in (2, 1, 3, 0):
            for half in range(2):
                self.bufs["y_out"][dx, pl.ds(half * h, h)] = self.product(1 - self.here.yl, dx, half).astype(BF16)
            self.y_copies[dx] = self.net.send(
                self.bufs["y_out"].at[dx], self.bufs["y_in"].at[dx], self.here.dev(dyl=1)
            )

    def second(self):
        self.ring.opposite()
        self.ring.beside()

    def third(self):
        self.ring.relay()

    def last(self):
        self.ring.arrive()

    def total(self, half):
        return self.ring.total(half)


class XFirst:
    def __init__(self, net, here, bufs, weight, acts, block):
        self.net, self.here, self.bufs, self.block = net, here, bufs, block
        self.weight, self.acts = weight, acts
        self.rings = [
            Ring(
                net, here, bufs["out"].at[i], bufs["far"].at[i], bufs["near"].at[i],
                functools.partial(self.product, row),
            )
            for i, row in enumerate((1 - here.yl, here.yl))
        ]

    product = YFirst.product

    def start(self):
        for ring in self.rings:
            ring.opposite()
        for ring in self.rings:
            ring.beside()

    def second(self):
        for ring in self.rings:
            ring.relay()

    def third(self):
        self.rings[0].arrive()
        h = self.block // 2
        for half in range(2):
            self.bufs["y_out"][0, pl.ds(half * h, h)] = self.rings[0].total(half).astype(BF16)
        self.y_copy = self.net.send(
            self.bufs["y_out"].at[0], self.bufs["y_in"].at[0], self.here.dev(dyl=1)
        )

    def last(self):
        self.rings[1].arrive()
        self.y_copy.wait_recv()

    def total(self, half):
        h = self.block // 2
        return self.rings[1].total(half) + self.bufs["y_in"][0, pl.ds(half * h, h)].astype(F32)


class Share:
    def __init__(self, net, here, buf, row, block):
        self.net, self.here, self.buf, self.row, self.block = net, here, buf, row, block
        self.h = block // 2
        self.right, self.left = here.dev(dx=1), here.dev(dx=3)

    def ref(self, dx, half=None):
        owner = self.here.owner(self.row, dx)
        if half is None:
            return self.buf.at[pl.ds(aligned(owner, self.block), self.block)]
        return self.buf.at[pl.ds(aligned(owner * 2 + half, self.h), self.h)]

    def push(self, ref, device):
        return self.net.send(ref, ref, device)

    def start(self):
        first = [self.push(self.ref(0, 0), self.right), self.push(self.ref(0, 1), self.left)]
        second = [self.push(self.ref(0, 1), self.right), self.push(self.ref(0, 0), self.left)]
        self.first, self.second = first, second

    def relay(self):
        self.first[0].wait_recv()
        self.far = [self.push(self.ref(3, 0), self.right)]
        self.first[1].wait_recv()
        self.far.append(self.push(self.ref(1, 1), self.left))

    def arrive_near(self):
        for copy in self.second:
            copy.wait_recv()

    def arrive_far(self):
        for copy in self.far:
            copy.wait_recv()


class ShareXFirst:
    def __init__(self, net, here, buf, block):
        self.net, self.here = net, here
        self.ring = Share(net, here, buf, here.yl, block)

    def over(self, dx):
        ref = self.ring.ref(dx)
        self.y_copies.append(self.net.send(ref, ref, self.here.dev(dyl=1)))

    def start(self):
        self.y_copies = []
        self.ring.start()
        self.over(0)

    def second(self):
        self.ring.relay()
        self.ring.arrive_near()
        self.over(1)
        self.over(3)

    def third(self):
        self.ring.arrive_far()
        self.over(2)

    def own_row(self):
        pass

    def other_row(self):
        for copy in self.y_copies:
            copy.wait_recv()


class ShareYFirst:
    def __init__(self, net, here, buf, block):
        self.net, self.here = net, here
        self.rings = [Share(net, here, buf, row, block) for row in (here.yl, 1 - here.yl)]

    def start(self):
        ref = self.rings[0].ref(0)
        self.y_copy = self.net.send(ref, ref, self.here.dev(dyl=1))
        self.rings[0].start()

    def second(self):
        self.y_copy.wait_recv()
        self.rings[1].start()
        self.rings[0].relay()

    def third(self):
        self.rings[1].relay()

    def own_row(self):
        self.rings[0].arrive_near()
        self.rings[0].arrive_far()

    def other_row(self):
        self.rings[1].arrive_near()
        self.rings[1].arrive_far()


class Chunk:
    def __init__(self, index, net, here, bufs, shared):
        self.first, self.size = CHUNKS[index]
        self.is_first, self.is_last = index == 0, index == len(CHUNKS) - 1
        self.net, self.here, self.bufs, self.shared = net, here, bufs, shared

    def feature_ref(self, zblock, core):
        return self.bufs["acts"].at[
            :, pl.ds(aligned(zblock, 96), 96), pl.ds(aligned(core, self.size), self.size)
        ]

    def pass_on(self, zblock, device):
        ref = self.feature_ref(zblock, self.here.c)
        return self.net.send(ref, ref, device)

    def load(self):
        here = self.here
        for i, name in enumerate(("inputs", "out_grad")):
            block = self.shared[name][pl.ds(self.first, self.size), :]
            self.bufs["acts"][
                i, pl.ds(aligned(here.gz, 96), 96), pl.ds(aligned(here.c, self.size), self.size)
            ] = block.T

    def gather_start(self):
        here = self.here
        self.y_copy = self.pass_on(here.gz, here.dev(dyh=1))
        self.z_copies = [self.pass_on(here.gz, here.dev(dz=dz)) for dz in (1, 3, 2)]
        self.core_copies = [self.pass_on(here.gz, here.dev(dc=1))]

    def gather_second(self):
        here = self.here
        self.y_copy.wait_recv()
        block = here.zblock(1, 0)
        self.z_copies += [self.pass_on(block, here.dev(dz=dz)) for dz in (1, 3, 2)]
        self.core_copies.append(self.pass_on(block, here.dev(dc=1)))

    def gather_third(self):
        here = self.here
        for i, copy in enumerate(self.z_copies):
            copy.wait_recv()
            block = here.zblock(i // 3, (3, 1, 2)[i % 3])
            self.core_copies.append(self.pass_on(block, here.dev(dc=1)))

    def gather_last(self):
        for copy in self.core_copies:
            copy.wait_recv()

    def sum_start(self):
        block = self.shared["block"]
        args = (self.net, self.here)
        acts = self.bufs["acts"]
        self.pre = YFirst(*args, self.bufs["pre"], self.shared["up_t"], acts.at[0], block)
        self.back = XFirst(*args, self.bufs["back"], self.shared["down"], acts.at[1], block)
        self.back.start()
        self.pre.start()

    def sum_second(self):
        self.back.second()
        self.pre.second()

    def sum_third(self):
        self.back.third()
        self.pre.third()

    def activate(self):
        self.back.last()
        self.pre.last()
        hidden, back = self.bufs["hidden"], self.bufs["hidden_back"]
        block = self.shared["block"]
        h = block // 2
        for half in range(2):
            hidden[pl.ds(half * h, h), :] = self.pre.total(half)
            back[pl.ds(half * h, h), :] = self.back.total(half)
        base = self.here.gy * block

        @pl.loop(0, block // 16)
        def _(i):
            rows = pl.ds(pl.multiple_of(i * 16, 16), 16)
            to = pl.ds(pl.multiple_of(base + i * 16, 16), 16)
            x = hidden[rows, :]
            t = jnp.tanh(gelu_scale * (x + cubic_term * x * x * x))
            deriv = 0.5 * (1.0 + t) + 0.5 * x * (1.0 - t * t) * gelu_scale * (1.0 + 3.0 * cubic_term * x * x)
            self.bufs["activation"][to, :] = (0.5 * x * (1.0 + t)).astype(BF16)
            self.bufs["pre_grad"][to, :] = (back[rows, :] * deriv).astype(BF16)

    def share_start(self):
        block = self.shared["block"]
        self.act_share = ShareXFirst(self.net, self.here, self.bufs["activation"], block)
        self.grad_share = ShareYFirst(self.net, self.here, self.bufs["pre_grad"], block)
        self.grad_share.start()
        self.act_share.start()

    def share_second(self):
        self.grad_share.second()
        self.act_share.second()

    def share_third(self):
        self.grad_share.third()
        self.act_share.third()

    def in_grad_rows(self, row, add):
        up, pre_grad, total = self.shared["up"], self.bufs["pre_grad"], self.bufs["in_grad"]
        cols = pl.ds(aligned(row, 768), 768)

        @pl.loop(0, 3)
        def _(i):
            rows = pl.ds(pl.multiple_of(i * 256, 256), 256)
            value = nn(up[rows, cols], pre_grad[cols, :])
            total[rows, :] = total[rows, :] + value if add else value

    def weight_grads(self, row):
        acts, pre_grad, activation = self.bufs["acts"], self.bufs["pre_grad"], self.bufs["activation"]
        shared = self.shared
        cols = pl.ds(aligned(row, 768), 768)

        def put(total, stage, rows, cols, value):
            if not self.is_first:
                value = value + total[rows, cols]
            if self.is_last:
                stage[rows, cols] = value.astype(BF16)
            else:
                total[rows, cols] = value

        @pl.loop(0, 3)
        def _(i):
            rows = pl.ds(pl.multiple_of(i * 256, 256), 256)
            put(
                shared["up_total"], shared["up_stage"], rows, cols,
                nt(acts[0, rows, :], pre_grad[cols, :]),
            )

        if self.is_last:
            part = (slice(None), cols)
            self.flush(shared["up_stage"].at[part], shared["up_grad"].at[part])

        @pl.loop(0, 3)
        def _(i):
            rows = pl.ds(pl.multiple_of(row * 768 + i * 256, 256), 256)
            put(
                shared["down_total"], shared["down_stage"], rows, slice(None),
                nt(activation[rows, :], acts[1]),
            )

        if self.is_last:
            self.flush(shared["down_stage"].at[cols], shared["down_grad"].at[cols])

    def flush(self, src, dst):
        i = len(self.shared["flushes"])
        copy = pltpu.make_async_copy(src, dst, self.shared["local_sems"].at[i])
        copy.start()
        self.shared["flushes"].append(copy)

    def reduce_start(self):
        here = self.here
        theirs = pl.ds(aligned(1 - here.c, self.size), self.size)
        self.core_copy = self.net.send(
            self.bufs["in_grad"].at[:, theirs], self.bufs["in_grad_core"], here.dev(dc=1)
        )

    def core_sum(self, zblock):
        rows = pl.ds(aligned(zblock, 96), 96)
        mine = pl.ds(aligned(self.here.c, self.size), self.size)
        return self.bufs["in_grad"][rows, mine] + self.bufs["in_grad_core"][rows, :]

    def reduce_second(self):
        here = self.here
        self.core_copy.wait_recv()
        self.reduce_copies = []
        offsets = [(dyh, dz) for dyh in (1, 0) for dz in (2, 1, 3, 0)][:-1]
        for i, (dyh, dz) in enumerate(offsets):
            src, dst = self.bufs["in_grad_out"].at[i], self.bufs["in_grad_in"].at[i]
            src[...] = self.core_sum(here.zblock(dyh, dz)).astype(BF16)
            self.reduce_copies.append(self.net.send(src, dst, here.dev(dyh=dyh, dz=dz)))

    def reduce_last(self):
        value = self.core_sum(self.here.gz)
        for i, copy in enumerate(self.reduce_copies):
            copy.wait_recv()
            value = value + self.bufs["in_grad_in"][i].astype(F32)
        self.shared["in_grad"][pl.ds(self.first, self.size), :] = value.T.astype(BF16)


def chunk_scratch(size, block):
    tokens = 2 * size
    h = block // 2
    sums = {
        "out": pltpu.VMEM((2, 3, block, tokens), BF16),
        "far": pltpu.VMEM((2, 2, h, tokens), BF16),
        "near": pltpu.VMEM((2, 2, block, tokens), BF16),
    }
    return {
        "acts": pltpu.VMEM((2, 768, tokens), BF16),
        "pre": {
            "out": pltpu.VMEM((1, 3, block, tokens), BF16),
            "far": pltpu.VMEM((1, 2, h, tokens), BF16),
            "near": pltpu.VMEM((1, 2, block, tokens), BF16),
            "y_out": pltpu.VMEM((4, block, tokens), BF16),
            "y_in": pltpu.VMEM((4, block, tokens), BF16),
        },
        "back": dict(
            sums,
            y_out=pltpu.VMEM((1, block, tokens), BF16),
            y_in=pltpu.VMEM((1, block, tokens), BF16),
        ),
        "hidden": pltpu.VMEM((block, tokens), F32),
        "hidden_back": pltpu.VMEM((block, tokens), F32),
        "activation": pltpu.VMEM((8 * block, tokens), BF16),
        "pre_grad": pltpu.VMEM((8 * block, tokens), BF16),
        "in_grad": pltpu.VMEM((768, tokens), F32),
        "in_grad_core": pltpu.VMEM((768, size), F32),
        "in_grad_out": pltpu.VMEM((7, 96, size), BF16),
        "in_grad_in": pltpu.VMEM((7, 96, size), BF16),
    }


def kernel(inputs, out_grad, up_hbm, down_hbm, in_grad, up_grad, down_grad, scratch):
    here = Place()
    net = Net(scratch["send_sems"], scratch["recv_sems"])
    local_sems = scratch["local_sems"]
    shared = dict(scratch["shared"])
    shared.update(
        inputs=inputs, out_grad=out_grad, in_grad=in_grad, up_grad=up_grad, down_grad=down_grad,
        block=192, local_sems=local_sems, flushes=[],
    )
    loads = [
        pltpu.make_async_copy(up_hbm, shared["up"], local_sems.at[4]),
        pltpu.make_async_copy(down_hbm, shared["down"], local_sems.at[5]),
    ]
    for copy in loads:
        copy.start()
    chunks = [Chunk(i, net, here, scratch["chunks"][i], shared) for i in range(len(CHUNKS))]
    for chunk in chunks:
        chunk.load()

    barrier = pltpu.get_barrier_semaphore()
    partners = [here.dev(dc=1), here.dev(dyl=1), here.dev(dx=1), here.dev(dx=3)]
    partners += [here.dev(dyh=dyh, dz=dz) for dyh in range(2) for dz in range(4) if dyh or dz]
    for device in partners:
        pl.semaphore_signal(barrier, inc=1, device_id=device, device_id_type=MESH)
    pl.semaphore_wait(barrier, len(partners))

    def turn(first, count):
        @pl.loop(first, first + count)
        def _(i):
            rows = pl.ds(pl.multiple_of(i * 128, 128), 128)
            shared["up_t"][rows, :] = shared["up"][:, rows].T

    first, rest = chunks[0], chunks[1:]
    first.gather_start()
    loads[0].wait()
    turn(0, 4)
    first.gather_second()
    turn(4, 8)
    first.gather_third()
    first.gather_last()
    loads[1].wait()
    first.sum_start()
    for i, chunk in enumerate(rest):
        before = chunks[i]
        chunk.gather_start()
        before.sum_second()
        chunk.gather_second()
        chunk.gather_third()
        before.sum_third()
        chunk.gather_last()
        chunk.sum_start()
        before.activate()
        before.share_start()
        if i:
            chunks[i - 1].share_second()
            chunks[i - 1].share_third()
            chunks[i - 1].finish()
    last = chunks[-1]
    last.sum_second()
    last.sum_third()
    if rest:
        before = chunks[-2]
        before.share_second()
    last.activate()
    last.share_start()
    if rest:
        before.share_third()
        before.grad_share.own_row()
        before.in_grad_rows(here.yl, False)
        before.weight_grads(here.yl)
    last.share_second()
    if rest:
        before.grad_share.other_row()
        before.in_grad_rows(1 - here.yl, True)
        before.reduce_start()
        before.act_share.other_row()
        before.weight_grads(1 - here.yl)
        before.reduce_second()
    last.share_third()
    last.grad_share.own_row()
    last.in_grad_rows(here.yl, False)
    last.weight_grads(here.yl)
    if rest:
        before.reduce_last()
    last.grad_share.other_row()
    last.in_grad_rows(1 - here.yl, True)
    last.reduce_start()
    last.act_share.other_row()
    last.reduce_second()
    last.weight_grads(1 - here.yl)
    last.reduce_last()
    for copy in shared["flushes"]:
        copy.wait()
    net.drain()


def body(inputs, out_grad, up_weight, down_weight):
    block = 192
    scratch = {
        "send_sems": pltpu.SemaphoreType.DMA((SEMS,)),
        "recv_sems": pltpu.SemaphoreType.DMA((SEMS,)),
        "local_sems": pltpu.SemaphoreType.DMA((6,)),
        "shared": {
            "up": pltpu.VMEM((768, 1536), BF16),
            "up_t": pltpu.VMEM((1536, 768), BF16),
            "down": pltpu.VMEM((1536, 768), BF16),
            "up_total": pltpu.VMEM((768, 1536), F32),
            "down_total": pltpu.VMEM((1536, 768), F32),
            "up_stage": pltpu.VMEM((768, 1536), BF16),
            "down_stage": pltpu.VMEM((1536, 768), BF16),
        },
        "chunks": [chunk_scratch(size, block) for _, size in CHUNKS],
    }
    leaves, tree = jax.tree.flatten(scratch)

    def run(*refs):
        kernel(*refs[:7], jax.tree.unflatten(tree, refs[7:]))

    vmem, hbm = pl.BlockSpec(memory_space=pltpu.VMEM), pl.BlockSpec(memory_space=pl.ANY)
    return pl.pallas_call(
        run,
        out_shape=(
            jax.ShapeDtypeStruct((640, 96), BF16),
            jax.ShapeDtypeStruct((768, 1536), BF16),
            jax.ShapeDtypeStruct((1536, 768), BF16),
        ),
        in_specs=[vmem, vmem, hbm, hbm],
        out_specs=(vmem, hbm, hbm),
        scratch_shapes=leaves,
        compiler_params=pltpu.CompilerParams(
            collective_id=0, has_side_effects=True, vmem_limit_bytes=63 * 2**20
        ),
        cost_estimate=pl.CostEstimate(
            flops=15_100_000_000, bytes_accessed=10_000_000, transcendentals=245_760
        ),
        name="mlp_backward",
    )(inputs, out_grad, up_weight, down_weight)


def solution(mesh):
    return jax.shard_map(
        body,
        mesh=mesh,
        in_specs=(
            P("gx", ("gy", "gz")),
            P("gx", ("gy", "gz")),
            P("gy", ("gx", "gz")),
            P(("gx", "gz"), "gy"),
        ),
        out_specs=(P("gx", ("gy", "gz")), P("gy", ("gx", "gz")), P(("gx", "gz"), "gy")),
        check_vma=False,
    )
```

```python
import functools

import jax
import jax.numpy as jnp
from jax import lax
from jax.experimental import pallas as pl
from jax.experimental.pallas import tpu as pltpu
from jax.sharding import PartitionSpec as P

gelu_scale = 0.7978845608028654
cubic_term = 0.044715

MESH = pl.DeviceIdType.MESH
BF16, F32 = jnp.bfloat16, jnp.float32

CHUNKS = ((0, 128), (128, 256), (384, 256))
SUMS = (('y', 'x'), ('y', 'x'), ('y', 'x'))
SHARES = (('x', 'y'), ('x', 'y'), ('y', 'y'))
REDUCES = ('z', 'z', 'direct')
SEMS = 90 * len(CHUNKS)
BLOCK = 192
HALF = 96
WIDTH = 768
ROW = 768

PLACES = ((2, 0), (2, 1), (1, 1), (3, 0), (1, 0), (3, 1), (0, 0), (0, 1))


def nn(left, right):
    return jnp.dot(left, right, preferred_element_type=F32)


def nt(left, right):
    return lax.dot_general(left, right, (((1,), (1,)), ((), ())), preferred_element_type=F32)


def aligned(index, step):
    return pl.multiple_of(index * step, step)


class Place:
    def __init__(self):
        self.c = lax.axis_index("gx")
        self.gy = lax.axis_index("gy")
        self.gz = lax.axis_index("gz")
        self.yl, self.x = self.gy // 4, self.gy % 4
        self.yh, self.z = self.gz // 4, self.gz % 4

    def dev(self, dc=0, dyl=0, dx=0, dyh=0, dz=0):
        return (
            (self.c + dc) % 2,
            self.owner((self.yl + dyl) % 2, dx),
            self.zblock(dyh, dz),
        )

    def owner(self, row, dx):
        return row * 4 + (self.x + dx) % 4

    def zblock(self, dyh, dz):
        return ((self.yh + dyh) % 2) * 4 + (self.z + dz) % 4


class Net:
    def __init__(self, send_sems, recv_sems):
        self.send_sems, self.recv_sems = send_sems, recv_sems
        self.copies = []

    def send(self, src, dst, device):
        i = len(self.copies)
        assert i < SEMS
        copy = pltpu.make_async_remote_copy(
            src_ref=src,
            dst_ref=dst,
            send_sem=self.send_sems.at[i],
            recv_sem=self.recv_sems.at[i],
            device_id=device,
            device_id_type=MESH,
        )
        copy.start()
        self.copies.append(copy)
        return copy

    def drain(self):
        for copy in self.copies:
            copy.wait_send()


class Ring:
    def __init__(self, net, here, out, far, near):
        self.net, self.out, self.far, self.near = net, out, far, near
        self.right, self.left = here.dev(dx=1), here.dev(dx=3)

    def push(self, place, dst, device):
        return self.net.send(self.out.at[pl.ds(place * HALF, HALF)], dst, device)

    def opposite(self):
        self.far_copies = [
            self.push(0, self.far.at[0], self.right), self.push(1, self.far.at[1], self.left)
        ]

    def beside(self):
        self.near_copies = [
            self.push(2, self.near.at[0, pl.ds(HALF, HALF)], self.right),
            self.push(3, self.near.at[1, pl.ds(0, HALF)], self.left),
        ]

    def relay(self, parts):
        for i, device in enumerate((self.right, self.left)):
            part = parts(i)
            self.far_copies[i].wait_recv()
            self.out[pl.ds((4 + i) * HALF, HALF)] = (part + self.far[i].astype(F32)).astype(BF16)
            self.near_copies.append(
                self.push(4 + i, self.near.at[i, pl.ds(i * HALF, HALF)], device)
            )

    def arrive(self):
        for copy in self.near_copies:
            copy.wait_recv()

    def add(self, part, half):
        rows = pl.ds(half * HALF, HALF)
        return part + self.near[0, rows].astype(F32) + self.near[1, rows].astype(F32)


class YFirst:
    def __init__(self, net, here, bufs, weight, acts):
        self.net, self.here, self.bufs = net, here, bufs
        self.weight, self.acts = weight, acts
        self.ring = Ring(net, here, bufs["out"].at[0], bufs["far"].at[0], bufs["near"].at[0])

    def start(self):
        y_out, y_in = self.bufs["y_out"], self.bufs["y_in"]
        self.y_copies = []
        for i in range(2):
            rows = pl.ds(i * 2 * BLOCK, 2 * BLOCK)
            y_out[rows] = nn(self.weight[rows], self.acts[...]).astype(BF16)
            for j in (2 * i, 2 * i + 1):
                rows = pl.ds(j * BLOCK, BLOCK)
                self.y_copies.append(self.net.send(y_out.at[rows], y_in.at[rows], self.here.dev(dyl=1)))

    def rest(self):
        for i in range(2):
            rows, weight_rows = pl.ds(i * 2 * BLOCK, 2 * BLOCK), pl.ds(ROW + i * 2 * BLOCK, 2 * BLOCK)
            self.bufs["held"][rows] = nn(self.weight[weight_rows], self.acts[...])

    def part(self, place):
        rows = pl.ds(place * HALF, HALF)
        return self.bufs["held"][rows] + self.bufs["y_in"][rows].astype(F32)

    def fill(self, i):
        self.y_copies[i].wait_recv()
        for place in (2 * i, 2 * i + 1):
            self.ring.out[pl.ds(place * HALF, HALF)] = self.part(place).astype(BF16)

    def first(self):
        self.fill(0)
        self.ring.opposite()

    def second(self):
        self.fill(1)
        self.ring.beside()

    def third(self):
        self.y_copies[2].wait_recv()
        self.ring.relay(lambda i: self.part(4 + i))

    def last(self):
        self.y_copies[3].wait_recv()
        self.ring.arrive()

    def total(self, half):
        return self.ring.add(self.part(6 + half), half)


class XFirst:
    def __init__(self, net, here, bufs, weight, acts):
        self.net, self.here, self.bufs = net, here, bufs
        self.weight, self.acts = weight, acts
        self.rings = [
            Ring(net, here, bufs["out"].at[i], bufs["far"].at[i], bufs["near"].at[i]) for i in range(2)
        ]

    def start(self):
        for i, ring in enumerate(self.rings):
            ring.out[pl.ds(0, 2 * BLOCK)] = nn(
                self.weight[pl.ds(i * ROW, 2 * BLOCK)], self.acts[...]
            ).astype(BF16)
            ring.opposite()
        for ring in self.rings:
            ring.beside()

    def rest(self):
        for i in range(2):
            self.bufs["held"][pl.ds(i * 2 * BLOCK, 2 * BLOCK)] = nn(
                self.weight[pl.ds(i * ROW + 2 * BLOCK, 2 * BLOCK)], self.acts[...]
            )

    def part(self, ring, place):
        return self.bufs["held"][pl.ds(ring * 2 * BLOCK + (place - 4) * HALF, HALF)]

    def first(self):
        self.rings[0].relay(lambda i: self.part(0, 4 + i))

    def second(self):
        self.rings[1].relay(lambda i: self.part(1, 4 + i))

    def third(self):
        self.rings[0].arrive()
        y_out, y_in = self.bufs["y_out"].at[pl.ds(0, BLOCK)], self.bufs["y_in"].at[pl.ds(0, BLOCK)]
        for half in range(2):
            y_out[pl.ds(half * HALF, HALF)] = self.rings[0].add(self.part(0, 6 + half), half).astype(BF16)
        self.y_copy = self.net.send(y_out, y_in, self.here.dev(dyl=1))

    def last(self):
        self.rings[1].arrive()
        self.y_copy.wait_recv()

    def total(self, half):
        rows = pl.ds(half * HALF, HALF)
        return self.rings[1].add(self.part(1, 6 + half), half) + self.bufs["y_in"][rows].astype(F32)


class Share:
    def __init__(self, net, here, buf, row, block):
        self.net, self.here, self.buf, self.row, self.block = net, here, buf, row, block
        self.h = block // 2
        self.right, self.left = here.dev(dx=1), here.dev(dx=3)

    def ref(self, dx, half=None):
        owner = self.here.owner(self.row, dx)
        if half is None:
            return self.buf.at[pl.ds(aligned(owner, self.block), self.block)]
        return self.buf.at[pl.ds(aligned(owner * 2 + half, self.h), self.h)]

    def push(self, ref, device):
        return self.net.send(ref, ref, device)

    def start(self):
        first = [self.push(self.ref(0, 0), self.right), self.push(self.ref(0, 1), self.left)]
        second = [self.push(self.ref(0, 1), self.right), self.push(self.ref(0, 0), self.left)]
        self.first, self.second = first, second

    def relay(self):
        self.first[0].wait_recv()
        self.far = [self.push(self.ref(3, 0), self.right)]
        self.first[1].wait_recv()
        self.far.append(self.push(self.ref(1, 1), self.left))

    def arrive_near(self):
        for copy in self.second:
            copy.wait_recv()

    def arrive_far(self):
        for copy in self.far:
            copy.wait_recv()


class ShareXFirst:
    def __init__(self, net, here, buf, block):
        self.net, self.here = net, here
        self.ring = Share(net, here, buf, here.yl, block)

    def over(self, dx):
        ref = self.ring.ref(dx)
        self.y_copies.append(self.net.send(ref, ref, self.here.dev(dyl=1)))

    def start(self):
        self.y_copies = []
        self.ring.start()
        self.over(0)

    def first(self):
        self.ring.relay()

    def second(self):
        self.ring.arrive_near()
        self.over(1)
        self.over(3)

    def third(self):
        self.ring.arrive_far()
        self.over(2)

    def own_row(self):
        pass

    def other_row(self):
        for copy in self.y_copies:
            copy.wait_recv()


class ShareYFirst:
    def __init__(self, net, here, buf, block):
        self.net, self.here = net, here
        self.rings = [Share(net, here, buf, row, block) for row in (here.yl, 1 - here.yl)]

    def start(self):
        ref = self.rings[0].ref(0)
        self.y_copy = self.net.send(ref, ref, self.here.dev(dyl=1))
        self.rings[0].start()

    def first(self):
        self.rings[0].relay()

    def second(self):
        self.y_copy.wait_recv()
        self.rings[1].start()

    def third(self):
        self.rings[1].relay()

    def own_row(self):
        self.rings[0].arrive_near()
        self.rings[0].arrive_far()

    def other_row(self):
        self.rings[1].arrive_near()
        self.rings[1].arrive_far()


class Chunk:
    def __init__(self, index, net, here, bufs, shared):
        self.first, self.size = CHUNKS[index]
        self.index = index
        self.is_first, self.is_last = index == 0, index == len(CHUNKS) - 1
        self.net, self.here, self.bufs, self.shared = net, here, bufs, shared

    def run(self, step):
        name, _, part = step.rpartition("_")
        if name in ("pre", "back", "act", "grad"):
            getattr(getattr(self, name), part)()
        else:
            getattr(self, step)()

    def feature_ref(self, zblock, core):
        return self.bufs["acts"].at[
            :, pl.ds(aligned(zblock, HALF), HALF), pl.ds(aligned(core, self.size), self.size)
        ]

    def pass_on(self, zblock, device):
        ref = self.feature_ref(zblock, self.here.c)
        return self.net.send(ref, ref, device)

    def load(self):
        here = self.here
        rows = pl.ds(aligned(here.gz, HALF), HALF)
        lanes = pl.ds(aligned(here.c, self.size), self.size)
        self.loads = []
        for i, name in enumerate(("inputs", "out_grad")):
            self.loads.append(
                self.shared["fetch"](
                    self.shared[name].at[:, pl.ds(self.first, self.size)],
                    self.bufs["acts"].at[i, rows, lanes],
                )
            )

    def gather_start(self):
        here = self.here
        for copy in self.loads:
            copy.wait()
        self.y_copy = self.pass_on(here.gz, here.dev(dyh=1))
        self.z_copies = [self.pass_on(here.gz, here.dev(dz=dz)) for dz in (1, 3, 2)]
        self.core_copies = [self.pass_on(here.gz, here.dev(dc=1))]

    def gather_second(self):
        here = self.here
        self.y_copy.wait_recv()
        block = here.zblock(1, 0)
        self.z_copies += [self.pass_on(block, here.dev(dz=dz)) for dz in (1, 3, 2)]
        self.core_copies.append(self.pass_on(block, here.dev(dc=1)))

    def gather_third(self):
        here = self.here
        for i in range(3):
            self.z_copies[i].wait_recv()
            self.core_copies.append(self.pass_on(here.zblock(0, (3, 1, 2)[i]), here.dev(dc=1)))

    def gather_fourth(self):
        here = self.here
        for i in range(3):
            self.z_copies[3 + i].wait_recv()
            self.core_copies.append(self.pass_on(here.zblock(1, (3, 1, 2)[i]), here.dev(dc=1)))

    def gather_last(self):
        for copy in self.core_copies:
            copy.wait_recv()

    def sum_start(self):
        acts = self.bufs["acts"]
        kinds = {"y": YFirst, "x": XFirst}
        sums = []
        for i, (name, weight) in enumerate((("pre", "up_t"), ("back", "down"))):
            kind = kinds[SUMS[self.index][i]]
            sums.append(kind(self.net, self.here, self.bufs[name], self.shared[weight], acts.at[i]))
        self.pre, self.back = sums
        self.back.start()
        self.pre.start()
        self.back.rest()
        self.pre.rest()

    def activate(self):
        self.back.last()
        self.pre.last()
        hidden, back = self.bufs["pre"]["held"], self.bufs["back"]["held"]
        at = 6 * HALF
        for half in range(2):
            rows = pl.ds(at + half * HALF, HALF)
            hidden[rows] = self.pre.total(half)
            back[rows] = self.back.total(half)
        base = self.here.gy * BLOCK

        @pl.loop(0, BLOCK // 16)
        def _(i):
            rows = pl.ds(pl.multiple_of(at + i * 16, 16), 16)
            to = pl.ds(pl.multiple_of(base + i * 16, 16), 16)
            x = hidden[rows, :]
            t = jnp.tanh(gelu_scale * (x + cubic_term * x * x * x))
            deriv = 0.5 * (1.0 + t) + 0.5 * x * (1.0 - t * t) * gelu_scale * (1.0 + 3.0 * cubic_term * x * x)
            self.bufs["activation"][to, :] = (0.5 * x * (1.0 + t)).astype(BF16)
            self.bufs["pre_grad"][to, :] = (back[rows, :] * deriv).astype(BF16)

        self.share_start()

    def share_start(self):
        kinds = {"x": ShareXFirst, "y": ShareYFirst}
        act, grad = SHARES[self.index]
        self.act_share = kinds[act](self.net, self.here, self.bufs["activation"], BLOCK)
        self.grad_share = kinds[grad](self.net, self.here, self.bufs["pre_grad"], BLOCK)
        self.grad, self.act = self.grad_share, self.act_share
        self.grad.start()
        self.act.start()

    def in_grad_rows(self, row, add):
        up, pre_grad, total = self.shared["up"], self.bufs["pre_grad"], self.bufs["in_grad"]
        cols = pl.ds(aligned(row, ROW), ROW)

        @pl.loop(0, 2)
        def _(i):
            rows = pl.ds(pl.multiple_of(i * 384, 384), 384)
            value = nn(up[rows, cols], pre_grad[cols, :])
            total[rows, :] = total[rows, :] + value if add else value

    def put(self, name, rows, cols, value):
        if not self.is_first:
            value = value + self.shared[name + "_total"][rows, cols]
        if self.is_last:
            self.shared[name + "_stage"][rows, cols] = value.astype(BF16)
        else:
            self.shared[name + "_total"][rows, cols] = value

    def up_rows(self, row):
        acts, pre_grad = self.bufs["acts"], self.bufs["pre_grad"]
        cols = pl.ds(aligned(row, ROW), ROW)

        @pl.loop(0, 2)
        def _(i):
            rows = pl.ds(pl.multiple_of(i * 384, 384), 384)
            self.put("up", rows, cols, nt(acts[0, rows, :], pre_grad[cols, :]))

        if self.is_last:
            part = (slice(None), cols)
            self.shared["flushes"].append(
                self.shared["fetch"](self.shared["up_stage"].at[part], self.shared["up_grad"].at[part])
            )

    def down_rows(self, row):
        acts, activation = self.bufs["acts"], self.bufs["activation"]

        @pl.loop(0, 2)
        def _(i):
            rows = pl.ds(pl.multiple_of(row * ROW + i * 384, 384), 384)
            self.put("down", rows, slice(None), nt(activation[rows, :], acts[1]))

        if self.is_last:
            part = pl.ds(aligned(row, ROW), ROW)
            self.shared["flushes"].append(
                self.shared["fetch"](self.shared["down_stage"].at[part], self.shared["down_grad"].at[part])
            )

    def in_grad_own(self):
        self.grad_share.own_row()
        self.in_grad_rows(self.here.yl, False)

    def in_grad_other(self):
        self.grad_share.other_row()
        self.in_grad_rows(1 - self.here.yl, True)
        self.reduce_start()

    def up_own(self):
        self.up_rows(self.here.yl)

    def up_other(self):
        self.up_rows(1 - self.here.yl)

    def down_own(self):
        self.act_share.own_row()
        self.down_rows(self.here.yl)

    def down_other(self):
        self.act_share.other_row()
        self.down_rows(1 - self.here.yl)

    def reduce_start(self):
        here = self.here
        theirs = pl.ds(aligned(1 - here.c, self.size), self.size)
        self.core_copy = self.net.send(
            self.bufs["in_grad"].at[:, theirs], self.bufs["in_grad_core"], here.dev(dc=1)
        )

    def core_sum(self, zblock):
        rows = pl.ds(aligned(zblock, HALF), HALF)
        mine = pl.ds(aligned(self.here.c, self.size), self.size)
        return self.bufs["in_grad"][rows, mine] + self.bufs["in_grad_core"][rows, :]

    def reduce_second(self):
        here = self.here
        self.core_copy.wait_recv()
        self.reduce_copies = []
        if REDUCES[self.index] == "direct":
            offsets = [(dyh, dz) for dyh in (1, 0) for dz in (2, 1, 3, 0)][:-1]
        else:
            offsets = [(dyh, dz) for dz in (2, 1, 3) for dyh in (1, 0)]
        for i, (dyh, dz) in enumerate(offsets):
            src, dst = self.bufs["in_grad_out"].at[i], self.bufs["in_grad_in"].at[i]
            src[...] = self.core_sum(here.zblock(dyh, dz)).astype(BF16)
            to = here.dev(dyh=dyh, dz=dz) if REDUCES[self.index] == "direct" else here.dev(dz=dz)
            self.reduce_copies.append(self.net.send(src, dst, to))

    def gathered(self, zblock, indices):
        value = self.core_sum(zblock)
        for i in indices:
            self.reduce_copies[i].wait_recv()
            value = value + self.bufs["in_grad_in"][i].astype(F32)
        return value

    def reduce_third(self):
        if REDUCES[self.index] == "direct":
            return
        src, dst = self.bufs["in_grad_out"].at[6], self.bufs["in_grad_in"].at[6]
        src[...] = self.gathered(self.here.zblock(1, 0), (0, 2, 4)).astype(BF16)
        self.reduce_copies.append(self.net.send(src, dst, self.here.dev(dyh=1)))

    def reduce_last(self):
        indices = range(7) if REDUCES[self.index] == "direct" else (1, 3, 5, 6)
        value = self.gathered(self.here.gz, indices)
        self.shared["in_grad"][:, pl.ds(self.first, self.size)] = value.astype(BF16)


ORDER = (
    "0.gather_start", "0.gather_second", "0.gather_third", "1.gather_start", "0.gather_fourth", "1.gather_second",
    "0.gather_last", "0.sum_start", "0.back_first", "1.gather_fourth", "1.gather_third", "2.gather_start",
    "0.back_second", "0.back_third", "1.gather_last", "1.sum_start", "0.pre_first", "1.back_first", "2.gather_third",
    "0.pre_second", "0.pre_third", "1.back_second", "2.gather_second", "0.activate", "2.gather_fourth",
    "2.gather_last", "2.sum_start", "0.act_first", "2.back_first", "1.pre_first", "2.back_second", "1.pre_second",
    "0.grad_second", "0.grad_first", "0.grad_third", "1.pre_third", "0.in_grad_own", "1.back_third", "2.pre_first",
    "2.pre_second", "1.activate", "0.in_grad_other", "2.pre_third", "0.reduce_second", "0.up_other", "0.reduce_third",
    "2.back_third", "1.grad_second", "1.grad_first", "1.act_first", "0.act_second", "2.activate", "1.grad_third",
    "0.reduce_last", "0.act_third", "1.in_grad_own", "2.grad_second", "1.act_second", "1.act_third",
    "1.in_grad_other", "2.grad_first", "0.up_own", "0.down_own", "1.up_other", "2.grad_third", "1.reduce_second",
    "1.up_own", "2.in_grad_own", "2.act_second", "2.in_grad_other", "0.down_other", "2.act_first", "1.down_own",
    "1.reduce_third", "2.reduce_second", "1.down_other", "2.act_third", "2.reduce_third", "1.reduce_last", "2.up_own",
    "2.up_other", "2.down_own", "2.down_other", "2.reduce_last",
)


def chunk_scratch(size, index):
    tokens = 2 * size

    def sums(rows, y_rows):
        return {
            "held": pltpu.VMEM((ROW, tokens), F32),
            "out": pltpu.VMEM((rows, 3 * BLOCK, tokens), BF16),
            "far": pltpu.VMEM((rows, 2, HALF, tokens), BF16),
            "near": pltpu.VMEM((rows, 2, BLOCK, tokens), BF16),
            "y_out": pltpu.VMEM((y_rows, tokens), BF16),
            "y_in": pltpu.VMEM((y_rows, tokens), BF16),
        }

    shapes = {"y": (1, ROW), "x": (2, BLOCK)}
    return {
        "acts": pltpu.VMEM((2, WIDTH, tokens), BF16),
        "pre": sums(*shapes[SUMS[index][0]]),
        "back": sums(*shapes[SUMS[index][1]]),
        "activation": pltpu.VMEM((8 * BLOCK, tokens), BF16),
        "pre_grad": pltpu.VMEM((8 * BLOCK, tokens), BF16),
        "in_grad": pltpu.VMEM((WIDTH, tokens), F32),
        "in_grad_core": pltpu.VMEM((WIDTH, size), F32),
        "in_grad_out": pltpu.VMEM((7, HALF, size), BF16),
        "in_grad_in": pltpu.VMEM((7, HALF, size), BF16),
    }


def kernel(inputs, out_grad, up_hbm, down_hbm, in_grad, up_grad, down_grad, scratch):
    here = Place()
    net = Net(scratch["send_sems"], scratch["recv_sems"])
    shared = dict(scratch["shared"])
    fetched = []

    def fetch(src, dst):
        copy = pltpu.make_async_copy(src, dst, scratch["local_sems"].at[len(fetched)])
        fetched.append(copy)
        copy.start()
        return copy

    shared.update(
        inputs=inputs, out_grad=out_grad, in_grad=in_grad, up_grad=up_grad, down_grad=down_grad,
        fetch=fetch, flushes=[],
    )
    chunks = [Chunk(i, net, here, scratch["chunks"][i], shared) for i in range(len(CHUNKS))]
    chunks[0].load()
    up_load = fetch(up_hbm, shared["up"])
    down_loads = []
    for row in range(2):
        for place, (dx, half) in enumerate(PLACES):
            first = aligned(here.owner((here.yl + 1 - row) % 2, dx) * 2 + half, HALF)
            down_loads.append(
                fetch(
                    down_hbm.at[pl.ds(first, HALF)],
                    shared["down"].at[pl.ds(row * ROW + place * HALF, HALF)],
                )
            )
    for chunk in chunks[1:]:
        chunk.load()

    natural = shared["down_stage"]

    def turn_up():
        for i in range(4):
            part = pl.ds(i * 384, 384)
            natural[part, :] = shared["up"][:, part].T

    def place_up():
        for row in range(2):
            for place, (dx, half) in enumerate(PLACES):
                source = aligned(here.owner((here.yl + 1 - row) % 2, dx) * 2 + half, HALF)
                shared["up_t"][pl.ds(row * ROW + place * HALF, HALF)] = natural[pl.ds(source, HALF)]

    barrier = pltpu.get_barrier_semaphore()
    partners = [here.dev(dc=1), here.dev(dyl=1), here.dev(dx=1), here.dev(dx=3)]
    partners += [here.dev(dyh=dyh, dz=dz) for dyh in range(2) for dz in range(4) if dyh or dz]
    for device in partners:
        pl.semaphore_signal(barrier, inc=1, device_id=device, device_id_type=MESH)
    pl.semaphore_wait(barrier, len(partners))

    for word in ORDER:
        chunk, step = chunks[int(word.split(".")[0])], word.split(".")[1]
        if word == "0.gather_second":
            up_load.wait()
            turn_up()
        if word == "0.gather_third":
            place_up()
        if word == "0.sum_start":
            for copy in down_loads:
                copy.wait()
        chunk.run(step)
    for copy in shared["flushes"]:
        copy.wait()
    net.drain()


def body(inputs, out_grad, up_weight, down_weight):
    scratch = {
        "send_sems": pltpu.SemaphoreType.DMA((SEMS,)),
        "recv_sems": pltpu.SemaphoreType.DMA((SEMS,)),
        "local_sems": pltpu.SemaphoreType.DMA((17 + 2 * len(CHUNKS) + 4,)),
        "shared": {
            "up": pltpu.VMEM((WIDTH, 2 * ROW), BF16),
            "up_t": pltpu.VMEM((2 * ROW, WIDTH), BF16),
            "down": pltpu.VMEM((2 * ROW, WIDTH), BF16),
            "up_total": pltpu.VMEM((WIDTH, 2 * ROW), F32),
            "down_total": pltpu.VMEM((2 * ROW, WIDTH), F32),
            "up_stage": pltpu.VMEM((WIDTH, 2 * ROW), BF16),
            "down_stage": pltpu.VMEM((2 * ROW, WIDTH), BF16),
        },
        "chunks": [chunk_scratch(size, i) for i, (_, size) in enumerate(CHUNKS)],
    }
    leaves, tree = jax.tree.flatten(scratch)

    def run(*refs):
        kernel(*refs[:7], jax.tree.unflatten(tree, refs[7:]))

    vmem, hbm = pl.BlockSpec(memory_space=pltpu.VMEM), pl.BlockSpec(memory_space=pl.ANY)
    in_grad, up_grad, down_grad = pl.pallas_call(
        run,
        out_shape=(
            jax.ShapeDtypeStruct((96, 640), BF16),
            jax.ShapeDtypeStruct((768, 1536), BF16),
            jax.ShapeDtypeStruct((1536, 768), BF16),
        ),
        in_specs=[hbm] * 4,
        out_specs=(vmem, hbm, hbm),
        scratch_shapes=leaves,
        compiler_params=pltpu.CompilerParams(
            collective_id=0, has_side_effects=True, vmem_limit_bytes=63 * 2**20
        ),
        cost_estimate=pl.CostEstimate(
            flops=15_100_000_000, bytes_accessed=10_000_000, transcendentals=245_760
        ),
        name="mlp_backward",
    )(inputs.T, out_grad.T, up_weight, down_weight)
    return in_grad.T, up_grad, down_grad


def solution(mesh):
    return jax.shard_map(
        body,
        mesh=mesh,
        in_specs=(
            P("gx", ("gy", "gz")),
            P("gx", ("gy", "gz")),
            P("gy", ("gx", "gz")),
            P(("gx", "gz"), "gy"),
        ),
        out_specs=(P("gx", ("gy", "gz")), P("gy", ("gx", "gz")), P(("gx", "gz"), "gy")),
        check_vma=False,
    )
```

```python
import functools

import jax
import jax.numpy as jnp
from jax import lax
from jax.experimental import pallas as pl
from jax.experimental.pallas import tpu as pltpu
from jax.sharding import PartitionSpec as P

gelu_scale = 0.7978845608028654
cubic_term = 0.044715

MESH = pl.DeviceIdType.MESH
BF16, F32 = jnp.bfloat16, jnp.float32

CHUNKS = ((0, 128), (128, 256), (384, 256))
SUMS = (("y", "x"), ("y", "x"), ("y", "x"))
SHARES = (("x", "y"), ("x", "y"), ("y", "y"))
REDUCES = ("z", "z", "direct")
SEND_SEMS = 7 * len(CHUNKS)
RECV_SEMS = sum(
    19 + sum({"x": 5, "y": 7}[kind] for kind in shares) + {"direct": 1, "z": 3}[reduce]
    for shares, reduce in zip(SHARES, REDUCES)
)
BLOCK = 192
HALF = 96
WIDTH = 768
ROW = 768

PLACES = ((2, 0), (2, 1), (1, 1), (3, 0), (1, 0), (3, 1), (0, 0), (0, 1))


def nn(left, right):
    return jnp.dot(left, right, preferred_element_type=F32)


def nt(left, right):
    return lax.dot_general(left, right, (((1,), (1,)), ((), ())), preferred_element_type=F32)


def aligned(index, step):
    return pl.multiple_of(index * step, step)


class Place:
    def __init__(self):
        self.c = lax.axis_index("gx")
        self.gy = lax.axis_index("gy")
        self.gz = lax.axis_index("gz")
        self.yl, self.x = self.gy // 4, self.gy % 4
        self.yh, self.z = self.gz // 4, self.gz % 4

    def dev(self, dc=0, dyl=0, dx=0, dyh=0, dz=0):
        return (
            (self.c + dc) % 2,
            self.owner((self.yl + dyl) % 2, dx),
            self.zblock(dyh, dz),
        )

    def owner(self, row, dx):
        return row * 4 + (self.x + dx) % 4

    def zblock(self, dyh, dz):
        return ((self.yh + dyh) % 2) * 4 + (self.z + dz) % 4


class Net:
    def __init__(self, send_sems, recv_sems):
        self.send_sems, self.recv_sems = send_sems, recv_sems
        self.outboxes, self.inboxes = 0, 0

    def outbox(self):
        assert self.outboxes < SEND_SEMS
        self.outboxes += 1
        return self.outboxes - 1

    def inbox(self):
        assert self.inboxes < RECV_SEMS
        self.inboxes += 1
        return self.inboxes - 1

    def send(self, src, dst, device, outbox, inbox):
        pltpu.make_async_remote_copy(
            src_ref=src,
            dst_ref=dst,
            send_sem=self.send_sems.at[outbox],
            recv_sem=self.recv_sems.at[inbox],
            device_id=device,
            device_id_type=MESH,
        ).start()

    def arrive(self, inbox, ref):
        pltpu.make_async_copy(ref, ref, self.recv_sems.at[inbox]).wait()

    def leave(self, outbox, ref):
        pltpu.make_async_copy(ref, ref, self.send_sems.at[outbox]).wait()


class Ring:
    def __init__(self, net, here, out, far, near, outbox):
        self.net, self.out, self.far, self.near, self.outbox = net, out, far, near, outbox
        self.far_boxes, self.near_box = (net.inbox(), net.inbox()), net.inbox()
        self.right, self.left = here.dev(dx=1), here.dev(dx=3)

    def push(self, place, dst, device, inbox):
        self.net.send(self.out.at[pl.ds(place * HALF, HALF)], dst, device, self.outbox, inbox)

    def opposite(self):
        self.push(0, self.far.at[0], self.right, self.far_boxes[0])
        self.push(1, self.far.at[1], self.left, self.far_boxes[1])

    def beside(self):
        self.push(2, self.near.at[0, pl.ds(HALF, HALF)], self.right, self.near_box)
        self.push(3, self.near.at[1, pl.ds(0, HALF)], self.left, self.near_box)

    def relay(self, parts):
        for i, device in enumerate((self.right, self.left)):
            part = parts(i)
            self.net.arrive(self.far_boxes[i], self.far.at[i])
            self.out[pl.ds((4 + i) * HALF, HALF)] = (part + self.far[i].astype(F32)).astype(BF16)
            self.push(4 + i, self.near.at[i, pl.ds(i * HALF, HALF)], device, self.near_box)

    def arrive(self):
        self.net.arrive(self.near_box, self.near)

    def add(self, part, half):
        rows = pl.ds(half * HALF, HALF)
        return part + self.near[0, rows].astype(F32) + self.near[1, rows].astype(F32)


class YFirst:
    def __init__(self, net, here, bufs, weight, acts):
        self.net, self.here, self.bufs = net, here, bufs
        self.weight, self.acts = weight, acts
        self.outbox = net.outbox()
        self.ring = Ring(net, here, bufs["out"].at[0], bufs["far"].at[0], bufs["near"].at[0], self.outbox)
        self.y_boxes = [net.inbox() for _ in range(4)]

    def start(self):
        y_out, y_in = self.bufs["y_out"], self.bufs["y_in"]
        for i in range(2):
            rows = pl.ds(i * 2 * BLOCK, 2 * BLOCK)
            y_out[rows] = nn(self.weight[rows], self.acts[...]).astype(BF16)
            for j in (2 * i, 2 * i + 1):
                rows = pl.ds(j * BLOCK, BLOCK)
                self.net.send(y_out.at[rows], y_in.at[rows], self.here.dev(dyl=1), self.outbox, self.y_boxes[j])

    def y_arrive(self, j):
        self.net.arrive(self.y_boxes[j], self.bufs["y_in"].at[pl.ds(j * BLOCK, BLOCK)])

    def rest(self):
        for i in range(2):
            rows, weight_rows = pl.ds(i * 2 * BLOCK, 2 * BLOCK), pl.ds(ROW + i * 2 * BLOCK, 2 * BLOCK)
            self.bufs["held"][rows] = nn(self.weight[weight_rows], self.acts[...])

    def part(self, place):
        rows = pl.ds(place * HALF, HALF)
        return self.bufs["held"][rows] + self.bufs["y_in"][rows].astype(F32)

    def fill(self, i):
        self.y_arrive(i)
        for place in (2 * i, 2 * i + 1):
            self.ring.out[pl.ds(place * HALF, HALF)] = self.part(place).astype(BF16)

    def first(self):
        self.fill(0)
        self.ring.opposite()

    def second(self):
        self.fill(1)
        self.ring.beside()

    def third(self):
        self.y_arrive(2)
        self.ring.relay(lambda i: self.part(4 + i))

    def last(self):
        self.y_arrive(3)
        self.ring.arrive()

    def total(self, half):
        return self.ring.add(self.part(6 + half), half)


class XFirst:
    def __init__(self, net, here, bufs, weight, acts):
        self.net, self.here, self.bufs = net, here, bufs
        self.weight, self.acts = weight, acts
        self.outbox, self.y_box = net.outbox(), net.inbox()
        self.rings = [
            Ring(net, here, bufs["out"].at[i], bufs["far"].at[i], bufs["near"].at[i], self.outbox)
            for i in range(2)
        ]

    def start(self):
        for i, ring in enumerate(self.rings):
            ring.out[pl.ds(0, 2 * BLOCK)] = nn(
                self.weight[pl.ds(i * ROW, 2 * BLOCK)], self.acts[...]
            ).astype(BF16)
            ring.opposite()
        for ring in self.rings:
            ring.beside()

    def rest(self):
        for i in range(2):
            self.bufs["held"][pl.ds(i * 2 * BLOCK, 2 * BLOCK)] = nn(
                self.weight[pl.ds(i * ROW + 2 * BLOCK, 2 * BLOCK)], self.acts[...]
            )

    def part(self, ring, place):
        return self.bufs["held"][pl.ds(ring * 2 * BLOCK + (place - 4) * HALF, HALF)]

    def first(self):
        self.rings[0].relay(lambda i: self.part(0, 4 + i))

    def second(self):
        self.rings[1].relay(lambda i: self.part(1, 4 + i))

    def third(self):
        self.rings[0].arrive()
        y_out, y_in = self.bufs["y_out"].at[pl.ds(0, BLOCK)], self.bufs["y_in"].at[pl.ds(0, BLOCK)]
        for half in range(2):
            y_out[pl.ds(half * HALF, HALF)] = self.rings[0].add(self.part(0, 6 + half), half).astype(BF16)
        self.net.send(y_out, y_in, self.here.dev(dyl=1), self.outbox, self.y_box)

    def last(self):
        self.rings[1].arrive()
        self.net.arrive(self.y_box, self.bufs["y_in"].at[pl.ds(0, BLOCK)])

    def total(self, half):
        rows = pl.ds(half * HALF, HALF)
        return self.rings[1].add(self.part(1, 6 + half), half) + self.bufs["y_in"][rows].astype(F32)


class Share:
    def __init__(self, net, here, buf, row, outbox, apart):
        self.net, self.here, self.buf, self.row, self.outbox = net, here, buf, row, outbox
        self.right, self.left = here.dev(dx=1), here.dev(dx=3)
        self.first_boxes, self.near_box = (net.inbox(), net.inbox()), net.inbox()
        self.far_box = net.inbox() if apart else self.near_box

    def ref(self, dx, half=None):
        owner = self.here.owner(self.row, dx)
        if half is None:
            return self.buf.at[pl.ds(aligned(owner, BLOCK), BLOCK)]
        return self.buf.at[pl.ds(aligned(owner * 2 + half, HALF), HALF)]

    def push(self, ref, device, inbox):
        self.net.send(ref, ref, device, self.outbox, inbox)

    def start(self):
        self.push(self.ref(0, 0), self.right, self.first_boxes[0])
        self.push(self.ref(0, 1), self.left, self.first_boxes[1])
        self.push(self.ref(0, 1), self.right, self.near_box)
        self.push(self.ref(0, 0), self.left, self.near_box)

    def relay(self):
        self.net.arrive(self.first_boxes[0], self.ref(3, 0))
        self.push(self.ref(3, 0), self.right, self.far_box)
        self.net.arrive(self.first_boxes[1], self.ref(1, 1))
        self.push(self.ref(1, 1), self.left, self.far_box)

    def arrive_near(self):
        self.net.arrive(self.near_box, self.ref(1))

    def arrive_far(self):
        self.net.arrive(self.far_box, self.ref(2))

    def arrive_all(self):
        self.net.arrive(self.near_box, self.buf.at[pl.ds(0, 2 * BLOCK)])


class ShareXFirst:
    def __init__(self, net, here, buf):
        self.net, self.here, self.buf = net, here, buf
        self.outbox, self.y_box = net.outbox(), net.inbox()
        self.ring = Share(net, here, buf, here.yl, self.outbox, True)

    def over(self, dx):
        ref = self.ring.ref(dx)
        self.net.send(ref, ref, self.here.dev(dyl=1), self.outbox, self.y_box)

    def start(self):
        self.ring.start()
        self.over(0)

    def first(self):
        self.ring.relay()

    def second(self):
        self.ring.arrive_near()
        self.over(1)
        self.over(3)

    def third(self):
        self.ring.arrive_far()
        self.over(2)

    def own_row(self):
        pass

    def other_row(self):
        self.net.arrive(self.y_box, self.buf.at[pl.ds(aligned(1 - self.here.yl, ROW), ROW)])


class ShareYFirst:
    def __init__(self, net, here, buf):
        self.net, self.here = net, here
        self.outbox, self.y_box = net.outbox(), net.inbox()
        self.rings = [Share(net, here, buf, row, self.outbox, False) for row in (here.yl, 1 - here.yl)]

    def start(self):
        ref = self.rings[0].ref(0)
        self.net.send(ref, ref, self.here.dev(dyl=1), self.outbox, self.y_box)
        self.rings[0].start()

    def first(self):
        self.rings[0].relay()

    def second(self):
        self.net.arrive(self.y_box, self.rings[1].ref(0))
        self.rings[1].start()

    def third(self):
        self.rings[1].relay()

    def own_row(self):
        self.rings[0].arrive_all()

    def other_row(self):
        self.rings[1].arrive_all()


class Chunk:
    def __init__(self, index, net, here, bufs, shared):
        self.first, self.size = CHUNKS[index]
        self.index = index
        self.is_first, self.is_last = index == 0, index == len(CHUNKS) - 1
        self.net, self.here, self.bufs, self.shared = net, here, bufs, shared
        sums, shares = {"y": YFirst, "x": XFirst}, {"x": ShareXFirst, "y": ShareYFirst}
        pre, back = (sums[kind] for kind in SUMS[index])
        act, grad = (shares[kind] for kind in SHARES[index])
        acts = bufs["acts"]
        self.pre = pre(net, here, bufs["pre"], shared["up_t"], acts.at[0])
        self.back = back(net, here, bufs["back"], shared["down"], acts.at[1])
        self.act = act(net, here, bufs["activation"])
        self.grad = grad(net, here, bufs["pre_grad"])
        self.gather_out, self.core_out, self.reduce_out = (net.outbox() for _ in range(3))
        self.y_box, self.z_boxes, self.core_box = net.inbox(), (net.inbox(), net.inbox()), net.inbox()
        self.in_grad_box = net.inbox()
        self.reduce_boxes = [net.inbox() for _ in range(1 if REDUCES[index] == "direct" else 3)]

    def feature_ref(self, zblock, core):
        return self.bufs["acts"].at[
            :, pl.ds(aligned(zblock, HALF), HALF), pl.ds(aligned(core, self.size), self.size)
        ]

    def pass_on(self, zblock, device, inbox):
        ref = self.feature_ref(zblock, self.here.c)
        self.net.send(ref, ref, device, self.gather_out, inbox)

    def load(self):
        here = self.here
        rows = pl.ds(aligned(here.gz, HALF), HALF)
        lanes = pl.ds(aligned(here.c, self.size), self.size)
        self.loads = []
        for i, name in enumerate(("inputs", "out_grad")):
            self.loads.append(
                self.shared["fetch"](
                    self.shared[name].at[:, pl.ds(self.first, self.size)],
                    self.bufs["acts"].at[i, rows, lanes],
                )
            )

    def gather_start(self):
        here = self.here
        for copy in self.loads:
            copy.wait()
        self.pass_on(here.gz, here.dev(dyh=1), self.y_box)
        for dz in (1, 3, 2):
            self.pass_on(here.gz, here.dev(dz=dz), self.z_boxes[0])
        self.pass_on(here.gz, here.dev(dc=1), self.core_box)

    def gather_second(self):
        here = self.here
        block = here.zblock(1, 0)
        self.net.arrive(self.y_box, self.feature_ref(block, here.c))
        for dz in (1, 3, 2):
            self.pass_on(block, here.dev(dz=dz), self.z_boxes[1])
        self.pass_on(block, here.dev(dc=1), self.core_box)

    def gathered_row(self, dyh):
        here = self.here
        self.net.arrive(self.z_boxes[dyh], self.bufs["acts"].at[:, pl.ds(0, 3 * HALF), pl.ds(0, self.size)])
        for dz in (3, 1, 2):
            self.pass_on(here.zblock(dyh, dz), here.dev(dc=1), self.core_box)

    def gather_third(self):
        if self.is_first:
            self.shared["turn_up"]()
        self.gathered_row(0)

    def gather_fourth(self):
        self.gathered_row(1)

    def gather_last(self):
        theirs = pl.ds(aligned(1 - self.here.c, self.size), self.size)
        self.net.arrive(self.core_box, self.bufs["acts"].at[:, :, theirs])
        if self.is_first:
            for copy in self.shared["down_loads"]:
                copy.wait()

    def activate(self):
        self.back.last()
        self.pre.last()
        hidden, back = self.bufs["pre"]["held"], self.bufs["back"]["held"]
        at = 6 * HALF
        for half in range(2):
            rows = pl.ds(at + half * HALF, HALF)
            hidden[rows] = self.pre.total(half)
            back[rows] = self.back.total(half)
        base = self.here.gy * BLOCK

        @pl.loop(0, BLOCK // 16)
        def _(i):
            rows = pl.ds(pl.multiple_of(at + i * 16, 16), 16)
            to = pl.ds(pl.multiple_of(base + i * 16, 16), 16)
            x = hidden[rows, :]
            t = jnp.tanh(gelu_scale * (x + cubic_term * x * x * x))
            deriv = 0.5 * (1.0 + t) + 0.5 * x * (1.0 - t * t) * gelu_scale * (1.0 + 3.0 * cubic_term * x * x)
            self.bufs["activation"][to, :] = (0.5 * x * (1.0 + t)).astype(BF16)
            self.bufs["pre_grad"][to, :] = (back[rows, :] * deriv).astype(BF16)

    def in_grad_rows(self, row, add):
        up, pre_grad, total = self.shared["up"], self.bufs["pre_grad"], self.bufs["in_grad"]
        cols = pl.ds(aligned(row, ROW), ROW)

        @pl.loop(0, 2)
        def _(i):
            rows = pl.ds(pl.multiple_of(i * 384, 384), 384)
            value = nn(up[rows, cols], pre_grad[cols, :])
            total[rows, :] = total[rows, :] + value if add else value

    def put(self, name, rows, cols, value):
        if not self.is_first:
            value = value + self.shared[name + "_total"][rows, cols]
        if self.is_last:
            self.shared[name + "_grad"][rows, cols] = value.astype(BF16)
        else:
            self.shared[name + "_total"][rows, cols] = value

    def up_rows(self, row):
        acts, pre_grad = self.bufs["acts"], self.bufs["pre_grad"]
        cols = pl.ds(aligned(row, ROW), ROW)

        @pl.loop(0, 2)
        def _(i):
            rows = pl.ds(pl.multiple_of(i * 384, 384), 384)
            self.put("up", rows, cols, nt(acts[0, rows, :], pre_grad[cols, :]))

    def down_rows(self, row):
        acts, activation = self.bufs["acts"], self.bufs["activation"]

        @pl.loop(0, 2)
        def _(i):
            rows = pl.ds(pl.multiple_of(row * ROW + i * 384, 384), 384)
            self.put("down", rows, slice(None), nt(activation[rows, :], acts[1]))

    def in_grad_own(self):
        self.grad.own_row()
        self.in_grad_rows(self.here.yl, False)

    def in_grad_other(self):
        self.grad.other_row()
        self.in_grad_rows(1 - self.here.yl, True)
        self.reduce_start()

    def up_own(self):
        self.up_rows(self.here.yl)

    def up_other(self):
        self.up_rows(1 - self.here.yl)

    def down_own(self):
        self.act.own_row()
        self.down_rows(self.here.yl)

    def down_other(self):
        self.act.other_row()
        self.down_rows(1 - self.here.yl)

    def reduce_start(self):
        theirs = pl.ds(aligned(1 - self.here.c, self.size), self.size)
        self.net.send(
            self.bufs["in_grad"].at[:, theirs], self.bufs["in_grad_core"], self.here.dev(dc=1),
            self.core_out, self.in_grad_box,
        )

    def core_sum(self, zblock):
        rows = pl.ds(aligned(zblock, HALF), HALF)
        mine = pl.ds(aligned(self.here.c, self.size), self.size)
        return self.bufs["in_grad"][rows, mine] + self.bufs["in_grad_core"][rows, :]

    def reduce_send(self, i, value, device, inbox):
        src, dst = self.bufs["in_grad_out"].at[i], self.bufs["in_grad_in"].at[i]
        src[...] = value.astype(BF16)
        self.net.send(src, dst, device, self.reduce_out, inbox)

    def reduce_second(self):
        here = self.here
        self.net.arrive(self.in_grad_box, self.bufs["in_grad_core"])
        if REDUCES[self.index] == "direct":
            offsets = [(dyh, dz) for dyh in (1, 0) for dz in (2, 1, 3, 0)][:-1]
            for i, (dyh, dz) in enumerate(offsets):
                value = self.core_sum(here.zblock(dyh, dz))
                self.reduce_send(i, value, here.dev(dyh=dyh, dz=dz), self.reduce_boxes[0])
            return
        for i, (dyh, dz) in enumerate([(dyh, dz) for dyh in (1, 0) for dz in (2, 1, 3)]):
            value = self.core_sum(here.zblock(dyh, dz))
            self.reduce_send(i, value, here.dev(dz=dz), self.reduce_boxes[1 - dyh])

    def gathered(self, zblock, boxes):
        value = self.core_sum(zblock)
        for box, first, count in boxes:
            self.net.arrive(self.reduce_boxes[box], self.bufs["in_grad_in"].at[pl.ds(first, count)])
            for i in range(first, first + count):
                value = value + self.bufs["in_grad_in"][i].astype(F32)
        return value

    def reduce_third(self):
        if REDUCES[self.index] == "direct":
            return
        value = self.gathered(self.here.zblock(1, 0), ((0, 0, 3),))
        self.reduce_send(6, value, self.here.dev(dyh=1), self.reduce_boxes[2])

    def reduce_last(self):
        boxes = ((0, 0, 7),) if REDUCES[self.index] == "direct" else ((1, 3, 3), (2, 6, 1))
        value = self.gathered(self.here.gz, boxes)
        self.shared["in_grad"][:, pl.ds(self.first, self.size)] = value.astype(BF16)

    def drain(self):
        bufs = self.bufs
        self.net.leave(self.gather_out, bufs["acts"].at[:, pl.ds(0, 15 * HALF // 2)])
        for part in (self.pre, self.back, self.act, self.grad):
            self.net.leave(part.outbox, bufs["activation"].at[pl.ds(0, 14 * HALF)])
        self.net.leave(self.core_out, bufs["in_grad_core"])
        self.net.leave(self.reduce_out, bufs["in_grad_in"])


def order(chunks):
    a, b, c = chunks
    return (
        a.gather_start, a.gather_second, b.gather_start, a.gather_third, a.gather_fourth, b.gather_second,
        c.gather_start, a.gather_last, a.back.start, a.pre.start, a.back.rest, a.pre.rest, a.pre.first,
        b.gather_third, a.back.first, a.pre.second, a.back.second, b.gather_fourth, a.back.third, a.pre.third,
        c.gather_second, b.gather_last, b.back.start, b.pre.start, a.activate, b.back.rest, b.pre.rest, b.back.first,
        a.grad.start, c.gather_third, c.gather_fourth, c.gather_last, c.back.start, c.pre.start, b.back.second,
        b.pre.first, b.pre.second, b.back.third, c.pre.rest, c.back.rest, a.grad.first, a.grad.second, b.pre.third,
        c.pre.first, c.back.first, c.pre.second, c.back.second, c.pre.third, c.back.third, b.activate, a.grad.third,
        b.grad.start, a.act.start, c.activate, b.act.start, b.grad.second, b.grad.first, a.in_grad_own, a.act.first,
        a.in_grad_other, c.grad.start, a.reduce_second, b.grad.third, a.act.second, b.in_grad_own, a.up_other,
        c.grad.second, a.act.third, b.act.first, b.act.second, c.grad.first, a.down_own, c.grad.third, c.act.start,
        b.in_grad_other, a.reduce_third, b.up_other, a.up_own, b.act.third, b.down_own, b.up_own, b.reduce_second,
        c.in_grad_own, c.in_grad_other, c.up_other, c.act.first, c.act.second, a.down_other, a.reduce_last,
        c.reduce_second, c.act.third, c.reduce_third, b.reduce_third, b.down_other, c.up_own, c.reduce_last,
        c.down_own, b.reduce_last, c.down_other,
    )


def chunk_scratch(size, index):
    tokens = 2 * size

    def sums(rows, y_rows):
        return {
            "held": pltpu.VMEM((ROW, tokens), F32),
            "out": pltpu.VMEM((rows, 3 * BLOCK, tokens), BF16),
            "far": pltpu.VMEM((rows, 2, HALF, tokens), BF16),
            "near": pltpu.VMEM((rows, 2, BLOCK, tokens), BF16),
            "y_out": pltpu.VMEM((y_rows, tokens), BF16),
            "y_in": pltpu.VMEM((y_rows, tokens), BF16),
        }

    shapes = {"y": (1, ROW), "x": (2, BLOCK)}
    return {
        "acts": pltpu.VMEM((2, WIDTH, tokens), BF16),
        "pre": sums(*shapes[SUMS[index][0]]),
        "back": sums(*shapes[SUMS[index][1]]),
        "activation": pltpu.VMEM((8 * BLOCK, tokens), BF16),
        "pre_grad": pltpu.VMEM((8 * BLOCK, tokens), BF16),
        "in_grad": pltpu.VMEM((WIDTH, tokens), F32),
        "in_grad_core": pltpu.VMEM((WIDTH, size), F32),
        "in_grad_out": pltpu.VMEM((7, HALF, size), BF16),
        "in_grad_in": pltpu.VMEM((7, HALF, size), BF16),
    }


def kernel(inputs, out_grad, up_hbm, down_hbm, in_grad, up_grad, down_grad, scratch):
    here = Place()
    net = Net(scratch["send_sems"], scratch["recv_sems"])
    shared = dict(scratch["shared"])
    fetched = []

    def fetch(src, dst):
        copy = pltpu.make_async_copy(src, dst, scratch["local_sems"].at[len(fetched)])
        fetched.append(copy)
        copy.start()
        return copy

    shared.update(
        inputs=inputs, out_grad=out_grad, in_grad=in_grad, up_grad=up_grad, down_grad=down_grad, fetch=fetch
    )
    chunks = [Chunk(i, net, here, scratch["chunks"][i], shared) for i in range(len(CHUNKS))]
    chunks[0].load()
    up_load = fetch(up_hbm, shared["up"])
    down_loads = []
    for row in range(2):
        for place, (dx, half) in enumerate(PLACES):
            first = aligned(here.owner((here.yl + 1 - row) % 2, dx) * 2 + half, HALF)
            down_loads.append(
                fetch(
                    down_hbm.at[pl.ds(first, HALF)],
                    shared["down"].at[pl.ds(row * ROW + place * HALF, HALF)],
                )
            )
    for chunk in chunks[1:]:
        chunk.load()

    natural = down_grad

    def turn_up():
        up_load.wait()
        for i in range(4):
            part = pl.ds(i * 384, 384)
            natural[part, :] = shared["up"][:, part].T
        for row in range(2):
            for place, (dx, half) in enumerate(PLACES):
                source = aligned(here.owner((here.yl + 1 - row) % 2, dx) * 2 + half, HALF)
                shared["up_t"][pl.ds(row * ROW + place * HALF, HALF)] = natural[pl.ds(source, HALF)]

    shared.update(turn_up=turn_up, down_loads=down_loads)
    barrier = pltpu.get_barrier_semaphore()
    partners = [here.dev(dc=1), here.dev(dyl=1), here.dev(dx=1), here.dev(dx=3)]
    partners += [here.dev(dyh=dyh, dz=dz) for dyh in range(2) for dz in range(4) if dyh or dz]
    for device in partners:
        pl.semaphore_signal(barrier, inc=1, device_id=device, device_id_type=MESH)
    pl.semaphore_wait(barrier, len(partners))

    for step in order(chunks):
        step()
    for chunk in chunks:
        chunk.drain()


def hand_over(*refs):
    sources, results, sems = refs[:3], refs[3:6], refs[6]
    copies = []
    for i, (source, result) in enumerate(zip(sources, results)):
        copy = pltpu.make_async_copy(source, result, sems.at[i])
        copy.start()
        copies.append(copy)
    for copy in copies:
        copy.wait()


def body(inputs, out_grad, up_weight, down_weight):
    scratch = {
        "send_sems": pltpu.SemaphoreType.DMA((SEND_SEMS,)),
        "recv_sems": pltpu.SemaphoreType.DMA((RECV_SEMS,)),
        "local_sems": pltpu.SemaphoreType.DMA((17 + 2 * len(CHUNKS),)),
        "shared": {
            "up": pltpu.VMEM((WIDTH, 2 * ROW), BF16),
            "up_t": pltpu.VMEM((2 * ROW, WIDTH), BF16),
            "down": pltpu.VMEM((2 * ROW, WIDTH), BF16),
            "up_total": pltpu.VMEM((WIDTH, 2 * ROW), F32),
            "down_total": pltpu.VMEM((2 * ROW, WIDTH), F32),
        },
        "chunks": [chunk_scratch(size, i) for i, (_, size) in enumerate(CHUNKS)],
    }
    leaves, tree = jax.tree.flatten(scratch)

    def run(*refs):
        kernel(*refs[:7], jax.tree.unflatten(tree, refs[7:]))

    vmem, hbm = pl.BlockSpec(memory_space=pltpu.VMEM), pl.BlockSpec(memory_space=pl.ANY)
    in_grad, up_grad, down_grad = pl.pallas_call(
        run,
        out_shape=(
            pltpu.VMEM((HALF, 640), BF16),
            pltpu.VMEM((WIDTH, 2 * ROW), BF16),
            pltpu.VMEM((2 * ROW, WIDTH), BF16),
        ),
        in_specs=[hbm] * 4,
        out_specs=(vmem, vmem, vmem),
        scratch_shapes=leaves,
        compiler_params=pltpu.CompilerParams(
            collective_id=0, has_side_effects=True, vmem_limit_bytes=59 * 2**20
        ),
        cost_estimate=pl.CostEstimate(
            flops=15_100_000_000, bytes_accessed=10_000_000, transcendentals=245_760
        ),
        name="mlp_backward",
    )(inputs.T, out_grad.T, up_weight, down_weight)
    in_grad, up_grad, down_grad = pl.pallas_call(
        hand_over,
        out_shape=[jax.ShapeDtypeStruct(a.shape, a.dtype) for a in (in_grad, up_grad, down_grad)],
        in_specs=[hbm] * 3,
        out_specs=[hbm] * 3,
        scratch_shapes=[pltpu.SemaphoreType.DMA((3,))],
        compiler_params=pltpu.CompilerParams(vmem_limit_bytes=2**20),
        name="hand_over",
    )(in_grad, up_grad, down_grad)
    return in_grad.T, up_grad, down_grad


def solution(mesh):
    return jax.shard_map(
        body,
        mesh=mesh,
        in_specs=(
            P("gx", ("gy", "gz")),
            P("gx", ("gy", "gz")),
            P("gy", ("gx", "gz")),
            P(("gx", "gz"), "gy"),
        ),
        out_specs=(P("gx", ("gy", "gz")), P("gy", ("gx", "gz")), P(("gx", "gz"), "gy")),
        check_vma=False,
    )
```

```python
import functools

import jax
import jax.numpy as jnp
from jax import lax
from jax.experimental import pallas as pl
from jax.experimental.pallas import tpu as pltpu
from jax.sharding import PartitionSpec as P

gelu_scale = 0.7978845608028654
cubic_term = 0.044715

MESH = pl.DeviceIdType.MESH
BF16, F32 = jnp.bfloat16, jnp.float32

CHUNKS = ((0, 128), (128, 256), (384, 256))
SUMS = (("y", "x"), ("y", "x"), ("y", "x"))
SHARES = (("x", "y"), ("x", "y"), ("y", "y"))
REDUCES = ("z", "z", "direct")
SEND_SEMS = 7 * len(CHUNKS) + 1
RECV_SEMS = 4 + sum(
    19 + sum({"x": 5, "y": 7}[kind] for kind in shares) + {"direct": 1, "z": 3}[reduce]
    for shares, reduce in zip(SHARES, REDUCES)
)
BLOCK = 192
HALF = 96
WIDTH = 768
ROW = 768

PLACES = ((2, 0), (2, 1), (1, 1), (3, 0), (1, 0), (3, 1), (0, 0), (0, 1))


def nn(left, right):
    return jnp.dot(left, right, preferred_element_type=F32)


def nt(left, right):
    return lax.dot_general(left, right, (((1,), (1,)), ((), ())), preferred_element_type=F32)


def aligned(index, step):
    return pl.multiple_of(index * step, step)


class Place:
    def __init__(self):
        self.c = lax.axis_index("gx")
        self.gy = lax.axis_index("gy")
        self.gz = lax.axis_index("gz")
        self.yl, self.x = self.gy // 4, self.gy % 4
        self.yh, self.z = self.gz // 4, self.gz % 4

    def dev(self, dc=0, dyl=0, dx=0, dyh=0, dz=0):
        return (
            (self.c + dc) % 2,
            self.owner((self.yl + dyl) % 2, dx),
            self.zblock(dyh, dz),
        )

    def owner(self, row, dx):
        return row * 4 + (self.x + dx) % 4

    def zblock(self, dyh, dz):
        return ((self.yh + dyh) % 2) * 4 + (self.z + dz) % 4


class Net:
    def __init__(self, send_sems, recv_sems):
        self.send_sems, self.recv_sems = send_sems, recv_sems
        self.outboxes, self.inboxes = 0, 0

    def outbox(self):
        assert self.outboxes < SEND_SEMS
        self.outboxes += 1
        return self.outboxes - 1

    def inbox(self):
        assert self.inboxes < RECV_SEMS
        self.inboxes += 1
        return self.inboxes - 1

    def send(self, src, dst, device, outbox, inbox):
        pltpu.make_async_remote_copy(
            src_ref=src,
            dst_ref=dst,
            send_sem=self.send_sems.at[outbox],
            recv_sem=self.recv_sems.at[inbox],
            device_id=device,
            device_id_type=MESH,
        ).start()

    def arrive(self, inbox, ref):
        pltpu.make_async_copy(ref, ref, self.recv_sems.at[inbox]).wait()

    def leave(self, outbox, ref):
        pltpu.make_async_copy(ref, ref, self.send_sems.at[outbox]).wait()


class Ring:
    def __init__(self, net, here, out, far, near, outbox):
        self.net, self.out, self.far, self.near, self.outbox = net, out, far, near, outbox
        self.far_boxes, self.near_box = (net.inbox(), net.inbox()), net.inbox()
        self.right, self.left = here.dev(dx=1), here.dev(dx=3)

    def push(self, place, dst, device, inbox):
        self.net.send(self.out.at[pl.ds(place * HALF, HALF)], dst, device, self.outbox, inbox)

    def opposite(self):
        self.push(0, self.far.at[0], self.right, self.far_boxes[0])
        self.push(1, self.far.at[1], self.left, self.far_boxes[1])

    def beside(self):
        self.push(2, self.near.at[0, pl.ds(HALF, HALF)], self.right, self.near_box)
        self.push(3, self.near.at[1, pl.ds(0, HALF)], self.left, self.near_box)

    def relay(self, parts):
        for i, device in enumerate((self.right, self.left)):
            part = parts(i)
            self.net.arrive(self.far_boxes[i], self.far.at[i])
            self.out[pl.ds((4 + i) * HALF, HALF)] = (part + self.far[i].astype(F32)).astype(BF16)
            self.push(4 + i, self.near.at[i, pl.ds(i * HALF, HALF)], device, self.near_box)

    def arrive(self):
        self.net.arrive(self.near_box, self.near)

    def add(self, part, half):
        rows = pl.ds(half * HALF, HALF)
        return part + self.near[0, rows].astype(F32) + self.near[1, rows].astype(F32)


class YFirst:
    def __init__(self, net, here, bufs, weight, acts):
        self.net, self.here, self.bufs = net, here, bufs
        self.weight, self.acts = weight, acts
        self.outbox = net.outbox()
        self.ring = Ring(net, here, bufs["out"].at[0], bufs["far"].at[0], bufs["near"].at[0], self.outbox)
        self.y_boxes = [net.inbox() for _ in range(4)]

    def start(self):
        y_out, y_in = self.bufs["y_out"], self.bufs["y_in"]
        for i in range(2):
            rows = pl.ds(i * 2 * BLOCK, 2 * BLOCK)
            y_out[rows] = nn(self.weight[rows], self.acts[...]).astype(BF16)
            for j in (2 * i, 2 * i + 1):
                rows = pl.ds(j * BLOCK, BLOCK)
                self.net.send(y_out.at[rows], y_in.at[rows], self.here.dev(dyl=1), self.outbox, self.y_boxes[j])

    def y_arrive(self, j):
        self.net.arrive(self.y_boxes[j], self.bufs["y_in"].at[pl.ds(j * BLOCK, BLOCK)])

    def rest(self):
        for i in range(2):
            rows, weight_rows = pl.ds(i * 2 * BLOCK, 2 * BLOCK), pl.ds(ROW + i * 2 * BLOCK, 2 * BLOCK)
            self.bufs["held"][rows] = nn(self.weight[weight_rows], self.acts[...])

    def part(self, place):
        rows = pl.ds(place * HALF, HALF)
        return self.bufs["held"][rows] + self.bufs["y_in"][rows].astype(F32)

    def fill(self, i):
        self.y_arrive(i)
        for place in (2 * i, 2 * i + 1):
            self.ring.out[pl.ds(place * HALF, HALF)] = self.part(place).astype(BF16)

    def first(self):
        self.fill(0)
        self.ring.opposite()

    def second(self):
        self.fill(1)
        self.ring.beside()

    def third(self):
        self.y_arrive(2)
        self.ring.relay(lambda i: self.part(4 + i))

    def last(self):
        self.y_arrive(3)
        self.ring.arrive()

    def total(self, half):
        return self.ring.add(self.part(6 + half), half)


class XFirst:
    def __init__(self, net, here, bufs, weight, acts):
        self.net, self.here, self.bufs = net, here, bufs
        self.weight, self.acts = weight, acts
        self.outbox, self.y_box = net.outbox(), net.inbox()
        self.rings = [
            Ring(net, here, bufs["out"].at[i], bufs["far"].at[i], bufs["near"].at[i], self.outbox)
            for i in range(2)
        ]

    def start(self):
        for i, ring in enumerate(self.rings):
            ring.out[pl.ds(0, 2 * BLOCK)] = nn(
                self.weight[pl.ds(i * ROW, 2 * BLOCK)], self.acts[...]
            ).astype(BF16)
            ring.opposite()
        for ring in self.rings:
            ring.beside()

    def rest(self):
        for i in range(2):
            self.bufs["held"][pl.ds(i * 2 * BLOCK, 2 * BLOCK)] = nn(
                self.weight[pl.ds(i * ROW + 2 * BLOCK, 2 * BLOCK)], self.acts[...]
            )

    def part(self, ring, place):
        return self.bufs["held"][pl.ds(ring * 2 * BLOCK + (place - 4) * HALF, HALF)]

    def first(self):
        self.rings[0].relay(lambda i: self.part(0, 4 + i))

    def second(self):
        self.rings[1].relay(lambda i: self.part(1, 4 + i))

    def third(self):
        self.rings[0].arrive()
        y_out, y_in = self.bufs["y_out"].at[pl.ds(0, BLOCK)], self.bufs["y_in"].at[pl.ds(0, BLOCK)]
        for half in range(2):
            y_out[pl.ds(half * HALF, HALF)] = self.rings[0].add(self.part(0, 6 + half), half).astype(BF16)
        self.net.send(y_out, y_in, self.here.dev(dyl=1), self.outbox, self.y_box)

    def last(self):
        self.rings[1].arrive()
        self.net.arrive(self.y_box, self.bufs["y_in"].at[pl.ds(0, BLOCK)])

    def total(self, half):
        rows = pl.ds(half * HALF, HALF)
        return self.rings[1].add(self.part(1, 6 + half), half) + self.bufs["y_in"][rows].astype(F32)


class Share:
    def __init__(self, net, here, buf, row, outbox, apart):
        self.net, self.here, self.buf, self.row, self.outbox = net, here, buf, row, outbox
        self.right, self.left = here.dev(dx=1), here.dev(dx=3)
        self.first_boxes, self.near_box = (net.inbox(), net.inbox()), net.inbox()
        self.far_box = net.inbox() if apart else self.near_box

    def ref(self, dx, half=None):
        owner = self.here.owner(self.row, dx)
        if half is None:
            return self.buf.at[pl.ds(aligned(owner, BLOCK), BLOCK)]
        return self.buf.at[pl.ds(aligned(owner * 2 + half, HALF), HALF)]

    def push(self, ref, device, inbox):
        self.net.send(ref, ref, device, self.outbox, inbox)

    def start(self):
        self.push(self.ref(0, 0), self.right, self.first_boxes[0])
        self.push(self.ref(0, 1), self.left, self.first_boxes[1])
        self.push(self.ref(0, 1), self.right, self.near_box)
        self.push(self.ref(0, 0), self.left, self.near_box)

    def relay(self):
        self.net.arrive(self.first_boxes[0], self.ref(3, 0))
        self.push(self.ref(3, 0), self.right, self.far_box)
        self.net.arrive(self.first_boxes[1], self.ref(1, 1))
        self.push(self.ref(1, 1), self.left, self.far_box)

    def arrive_near(self):
        self.net.arrive(self.near_box, self.ref(1))

    def arrive_far(self):
        self.net.arrive(self.far_box, self.ref(2))

    def arrive_all(self):
        self.net.arrive(self.near_box, self.buf.at[pl.ds(0, 2 * BLOCK)])


class ShareXFirst:
    def __init__(self, net, here, buf):
        self.net, self.here, self.buf = net, here, buf
        self.outbox, self.y_box = net.outbox(), net.inbox()
        self.ring = Share(net, here, buf, here.yl, self.outbox, True)

    def over(self, dx):
        ref = self.ring.ref(dx)
        self.net.send(ref, ref, self.here.dev(dyl=1), self.outbox, self.y_box)

    def start(self):
        self.ring.start()
        self.over(0)

    def first(self):
        self.ring.relay()

    def second(self):
        self.ring.arrive_near()
        self.over(1)
        self.over(3)

    def third(self):
        self.ring.arrive_far()
        self.over(2)

    def own_row(self):
        pass

    def other_row(self):
        self.net.arrive(self.y_box, self.buf.at[pl.ds(aligned(1 - self.here.yl, ROW), ROW)])


class ShareYFirst:
    def __init__(self, net, here, buf):
        self.net, self.here = net, here
        self.outbox, self.y_box = net.outbox(), net.inbox()
        self.rings = [Share(net, here, buf, row, self.outbox, False) for row in (here.yl, 1 - here.yl)]

    def start(self):
        ref = self.rings[0].ref(0)
        self.net.send(ref, ref, self.here.dev(dyl=1), self.outbox, self.y_box)
        self.rings[0].start()

    def first(self):
        self.rings[0].relay()

    def second(self):
        self.net.arrive(self.y_box, self.rings[1].ref(0))
        self.rings[1].start()

    def third(self):
        self.rings[1].relay()

    def own_row(self):
        self.rings[0].arrive_all()

    def other_row(self):
        self.rings[1].arrive_all()


class Gather:
    def __init__(self, net, here, acts, size, first, count, ready):
        self.net, self.here, self.size, self.ready = net, here, size, ready
        self.acts = acts.at[pl.ds(first, count)]
        self.outbox, self.y_box = net.outbox(), net.inbox()
        self.z_boxes, self.core_box = (net.inbox(), net.inbox()), net.inbox()

    def feature_ref(self, zblock):
        rows = pl.ds(aligned(zblock, HALF), HALF)
        return self.acts.at[:, rows, pl.ds(aligned(self.here.c, self.size), self.size)]

    def pass_on(self, zblock, device, inbox):
        ref = self.feature_ref(zblock)
        self.net.send(ref, ref, device, self.outbox, inbox)

    def start(self):
        here = self.here
        self.ready()
        self.pass_on(here.gz, here.dev(dyh=1), self.y_box)
        for dz in (1, 3, 2):
            self.pass_on(here.gz, here.dev(dz=dz), self.z_boxes[0])
        self.pass_on(here.gz, here.dev(dc=1), self.core_box)

    def second(self):
        here = self.here
        block = here.zblock(1, 0)
        self.net.arrive(self.y_box, self.feature_ref(block))
        for dz in (1, 3, 2):
            self.pass_on(block, here.dev(dz=dz), self.z_boxes[1])
        self.pass_on(block, here.dev(dc=1), self.core_box)

    def row(self, dyh):
        here = self.here
        self.net.arrive(self.z_boxes[dyh], self.acts.at[:, pl.ds(0, 3 * HALF), pl.ds(0, self.size)])
        for dz in (3, 1, 2):
            self.pass_on(here.zblock(dyh, dz), here.dev(dc=1), self.core_box)

    def third(self):
        self.row(0)

    def fourth(self):
        self.row(1)

    def last(self):
        theirs = pl.ds(aligned(1 - self.here.c, self.size), self.size)
        self.net.arrive(self.core_box, self.acts.at[:, :, theirs])

    def drain(self):
        self.net.leave(self.outbox, self.acts.at[:, pl.ds(0, 15 * HALF // 2)])


class Chunk:
    def __init__(self, index, net, here, bufs, shared):
        self.first, self.size = CHUNKS[index]
        self.index = index
        self.is_first, self.is_last = index == 0, index == len(CHUNKS) - 1
        self.net, self.here, self.bufs, self.shared = net, here, bufs, shared
        sums, shares = {"y": YFirst, "x": XFirst}, {"x": ShareXFirst, "y": ShareYFirst}
        pre, back = (sums[kind] for kind in SUMS[index])
        act, grad = (shares[kind] for kind in SHARES[index])
        acts = bufs["acts"]
        self.pre = pre(net, here, bufs["pre"], shared["up_t"], acts.at[0])
        self.back = back(net, here, bufs["back"], shared["down"], acts.at[1])
        self.act = act(net, here, bufs["activation"])
        self.grad = grad(net, here, bufs["pre_grad"])
        if self.is_first:
            self.feat = Gather(net, here, acts, self.size, 1, 1, self.ready)
            self.feat_two = Gather(net, here, acts, self.size, 0, 1, lambda: None)
        else:
            self.feat = self.feat_two = Gather(net, here, acts, self.size, 0, 2, self.ready)
        self.core_out, self.reduce_out = net.outbox(), net.outbox()
        self.in_grad_box = net.inbox()
        self.reduce_boxes = [net.inbox() for _ in range(1 if REDUCES[index] == "direct" else 3)]

    def ready(self):
        for copy in self.loads:
            copy.wait()

    def load(self):
        here = self.here
        rows = pl.ds(aligned(here.gz, HALF), HALF)
        lanes = pl.ds(aligned(here.c, self.size), self.size)
        self.loads = []
        for i, name in enumerate(("inputs", "out_grad")):
            self.loads.append(
                self.shared["fetch"](
                    self.shared[name].at[:, pl.ds(self.first, self.size)],
                    self.bufs["acts"].at[i, rows, lanes],
                )
            )

    def activate(self):
        self.back.last()
        self.pre.last()
        hidden, back = self.bufs["pre"]["held"], self.bufs["back"]["held"]
        at = 6 * HALF
        for half in range(2):
            rows = pl.ds(at + half * HALF, HALF)
            hidden[rows] = self.pre.total(half)
            back[rows] = self.back.total(half)
        base = self.here.gy * BLOCK

        @pl.loop(0, BLOCK // 16)
        def _(i):
            rows = pl.ds(pl.multiple_of(at + i * 16, 16), 16)
            to = pl.ds(pl.multiple_of(base + i * 16, 16), 16)
            x = hidden[rows, :]
            t = jnp.tanh(gelu_scale * (x + cubic_term * x * x * x))
            deriv = 0.5 * (1.0 + t) + 0.5 * x * (1.0 - t * t) * gelu_scale * (1.0 + 3.0 * cubic_term * x * x)
            self.bufs["activation"][to, :] = (0.5 * x * (1.0 + t)).astype(BF16)
            self.bufs["pre_grad"][to, :] = (back[rows, :] * deriv).astype(BF16)

    def in_grad_rows(self, row, add):
        up, pre_grad, total = self.shared["up"], self.bufs["pre_grad"], self.bufs["in_grad"]
        cols = pl.ds(aligned(row, ROW), ROW)

        @pl.loop(0, 2)
        def _(i):
            rows = pl.ds(pl.multiple_of(i * 384, 384), 384)
            value = nn(up[rows, cols], pre_grad[cols, :])
            total[rows, :] = total[rows, :] + value if add else value

    def put(self, name, rows, cols, value):
        if not self.is_first:
            value = value + self.shared[name + "_total"][rows, cols]
        if self.is_last:
            self.shared[name + "_grad"][rows, cols] = value.astype(BF16)
        else:
            self.shared[name + "_total"][rows, cols] = value

    def up_rows(self, row):
        acts, pre_grad = self.bufs["acts"], self.bufs["pre_grad"]
        cols = pl.ds(aligned(row, ROW), ROW)

        @pl.loop(0, 2)
        def _(i):
            rows = pl.ds(pl.multiple_of(i * 384, 384), 384)
            self.put("up", rows, cols, nt(acts[0, rows, :], pre_grad[cols, :]))

    def down_rows(self, row):
        acts, activation = self.bufs["acts"], self.bufs["activation"]

        @pl.loop(0, 2)
        def _(i):
            rows = pl.ds(pl.multiple_of(row * ROW + i * 384, 384), 384)
            self.put("down", rows, slice(None), nt(activation[rows, :], acts[1]))

    def prepare(self):
        if self.is_first:
            self.shared["turn_up"]()
            self.shared["turn_down"]()

    def in_grad_own(self):
        self.grad.own_row()
        self.in_grad_rows(self.here.yl, False)

    def in_grad_other(self):
        self.grad.other_row()
        self.in_grad_rows(1 - self.here.yl, True)
        self.reduce_start()

    def up_own(self):
        self.up_rows(self.here.yl)

    def up_other(self):
        self.up_rows(1 - self.here.yl)

    def down_own(self):
        self.act.own_row()
        self.down_rows(self.here.yl)

    def down_other(self):
        self.act.other_row()
        self.down_rows(1 - self.here.yl)

    def reduce_start(self):
        theirs = pl.ds(aligned(1 - self.here.c, self.size), self.size)
        self.net.send(
            self.bufs["in_grad"].at[:, theirs], self.bufs["in_grad_core"], self.here.dev(dc=1),
            self.core_out, self.in_grad_box,
        )

    def core_sum(self, zblock):
        rows = pl.ds(aligned(zblock, HALF), HALF)
        mine = pl.ds(aligned(self.here.c, self.size), self.size)
        return self.bufs["in_grad"][rows, mine] + self.bufs["in_grad_core"][rows, :]

    def reduce_send(self, i, value, device, inbox):
        src, dst = self.bufs["in_grad_out"].at[i], self.bufs["in_grad_in"].at[i]
        src[...] = value.astype(BF16)
        self.net.send(src, dst, device, self.reduce_out, inbox)

    def reduce_second(self):
        here = self.here
        self.net.arrive(self.in_grad_box, self.bufs["in_grad_core"])
        if REDUCES[self.index] == "direct":
            offsets = [(dyh, dz) for dyh in (1, 0) for dz in (2, 1, 3, 0)][:-1]
            for i, (dyh, dz) in enumerate(offsets):
                value = self.core_sum(here.zblock(dyh, dz))
                self.reduce_send(i, value, here.dev(dyh=dyh, dz=dz), self.reduce_boxes[0])
            return
        for i, (dyh, dz) in enumerate([(dyh, dz) for dyh in (1, 0) for dz in (2, 1, 3)]):
            value = self.core_sum(here.zblock(dyh, dz))
            self.reduce_send(i, value, here.dev(dz=dz), self.reduce_boxes[1 - dyh])

    def gathered(self, zblock, boxes):
        value = self.core_sum(zblock)
        for box, first, count in boxes:
            self.net.arrive(self.reduce_boxes[box], self.bufs["in_grad_in"].at[pl.ds(first, count)])
            for i in range(first, first + count):
                value = value + self.bufs["in_grad_in"][i].astype(F32)
        return value

    def reduce_third(self):
        if REDUCES[self.index] == "direct":
            return
        value = self.gathered(self.here.zblock(1, 0), ((0, 0, 3),))
        self.reduce_send(6, value, self.here.dev(dyh=1), self.reduce_boxes[2])

    def reduce_last(self):
        boxes = ((0, 0, 7),) if REDUCES[self.index] == "direct" else ((1, 3, 3), (2, 6, 1))
        value = self.gathered(self.here.gz, boxes)
        self.shared["in_grad"][:, pl.ds(self.first, self.size)] = value.astype(BF16)

    def drain(self):
        bufs = self.bufs
        self.feat.drain()
        if self.is_first:
            self.feat_two.drain()
        for part in (self.pre, self.back, self.act, self.grad):
            self.net.leave(part.outbox, bufs["activation"].at[pl.ds(0, 14 * HALF)])
        self.net.leave(self.core_out, bufs["in_grad_core"])
        self.net.leave(self.reduce_out, bufs["in_grad_in"])


def order(chunks):
    a, b, c = chunks
    return (
        a.feat.start, a.feat_two.start, a.feat.second, a.feat_two.second, b.feat.start, a.feat.third, a.prepare,
        a.feat.fourth, a.feat_two.fourth, a.feat_two.third, a.feat.last, b.feat.second, c.feat.start, a.back.start,
        a.feat_two.last, a.pre.start, a.back.rest, b.feat.third, a.back.first, a.pre.rest, a.back.second, a.pre.first,
        b.feat.fourth, c.feat.second, a.pre.second, a.back.third, b.feat.last, b.back.start, b.pre.start,
        c.feat.fourth, b.back.rest, c.feat.third, a.pre.third, b.back.first, b.back.second, a.activate, b.pre.rest,
        a.grad.start, b.pre.second, b.back.third, c.feat.last, c.back.start, c.back.rest, a.grad.first, b.pre.first,
        a.grad.second, a.act.start, c.back.second, c.pre.start, c.pre.rest, a.grad.third, a.in_grad_own, b.pre.third,
        c.pre.second, c.pre.first, a.act.first, a.in_grad_other, b.activate, c.back.first, b.grad.start, a.act.second,
        c.back.third, c.pre.third, b.act.start, b.grad.second, a.reduce_second, b.grad.first, a.act.third, a.down_own,
        a.reduce_third, c.activate, b.grad.third, a.up_own, b.act.first, a.up_other, c.grad.start, b.act.second,
        b.in_grad_own, b.in_grad_other, a.down_other, a.reduce_last, c.grad.second, b.reduce_second, b.up_other,
        c.grad.first, c.grad.third, b.reduce_third, c.act.start, b.up_own, c.in_grad_own, b.reduce_last, b.act.third,
        c.in_grad_other, c.act.first, b.down_own, c.act.second, c.reduce_second, c.reduce_third, c.up_other, c.up_own,
        c.act.third, b.down_other, c.down_own, c.reduce_last, c.down_other,
    )


def chunk_scratch(size, index):
    tokens = 2 * size

    def sums(rows, y_rows):
        return {
            "held": pltpu.VMEM((ROW, tokens), F32),
            "out": pltpu.VMEM((rows, 3 * BLOCK, tokens), BF16),
            "far": pltpu.VMEM((rows, 2, HALF, tokens), BF16),
            "near": pltpu.VMEM((rows, 2, BLOCK, tokens), BF16),
            "y_out": pltpu.VMEM((y_rows, tokens), BF16),
            "y_in": pltpu.VMEM((y_rows, tokens), BF16),
        }

    shapes = {"y": (1, ROW), "x": (2, BLOCK)}
    return {
        "acts": pltpu.VMEM((2, WIDTH, tokens), BF16),
        "pre": sums(*shapes[SUMS[index][0]]),
        "back": sums(*shapes[SUMS[index][1]]),
        "activation": pltpu.VMEM((8 * BLOCK, tokens), BF16),
        "pre_grad": pltpu.VMEM((8 * BLOCK, tokens), BF16),
        "in_grad": pltpu.VMEM((WIDTH, tokens), F32),
        "in_grad_core": pltpu.VMEM((WIDTH, size), F32),
        "in_grad_out": pltpu.VMEM((7, HALF, size), BF16),
        "in_grad_in": pltpu.VMEM((7, HALF, size), BF16),
    }


def kernel(inputs, out_grad, up_hbm, down_hbm, in_grad, up_grad, down_grad, scratch):
    here = Place()
    net = Net(scratch["send_sems"], scratch["recv_sems"])
    shared = dict(scratch["shared"])
    fetched = []

    def fetch(src, dst):
        copy = pltpu.make_async_copy(src, dst, scratch["local_sems"].at[len(fetched)])
        fetched.append(copy)
        copy.start()
        return copy

    shared.update(
        inputs=inputs, out_grad=out_grad, in_grad=in_grad, up_grad=up_grad, down_grad=down_grad, fetch=fetch
    )
    chunks = [Chunk(i, net, here, scratch["chunks"][i], shared) for i in range(len(CHUNKS))]
    chunks[0].load()
    up_load = fetch(up_hbm, shared["up"])
    down_loads = []
    for row in range(2):
        for place, (dx, half) in enumerate(PLACES):
            first = aligned(here.owner((here.yl + 1 - row) % 2, dx) * 2 + half, HALF)
            down_loads.append(
                fetch(
                    down_hbm.at[pl.ds(first, HALF)],
                    shared["down"].at[pl.ds(row * ROW + place * HALF, HALF)],
                )
            )
    for chunk in chunks[1:]:
        chunk.load()

    natural = down_grad

    def turn_down():
        for copy in down_loads:
            copy.wait()

    def turn_up():
        up_load.wait()
        for i in range(4):
            part = pl.ds(i * 384, 384)
            natural[part, :] = shared["up"][:, part].T
        for row in range(2):
            for place, (dx, half) in enumerate(PLACES):
                source = aligned(here.owner((here.yl + 1 - row) % 2, dx) * 2 + half, HALF)
                shared["up_t"][pl.ds(row * ROW + place * HALF, HALF)] = natural[pl.ds(source, HALF)]

    shared.update(turn_up=turn_up, turn_down=turn_down)
    barrier = pltpu.get_barrier_semaphore()
    partners = [here.dev(dc=1), here.dev(dyl=1), here.dev(dx=1), here.dev(dx=3)]
    partners += [here.dev(dyh=dyh, dz=dz) for dyh in range(2) for dz in range(4) if dyh or dz]
    for device in partners:
        pl.semaphore_signal(barrier, inc=1, device_id=device, device_id_type=MESH)
    pl.semaphore_wait(barrier, len(partners))

    for step in order(chunks):
        step()
    for chunk in chunks:
        chunk.drain()


def hand_over(*refs):
    sources, results, sems = refs[:3], refs[3:6], refs[6]
    copies = []
    for i, (source, result) in enumerate(zip(sources, results)):
        copy = pltpu.make_async_copy(source, result, sems.at[i])
        copy.start()
        copies.append(copy)
    for copy in copies:
        copy.wait()


def body(inputs, out_grad, up_weight, down_weight):
    scratch = {
        "send_sems": pltpu.SemaphoreType.DMA((SEND_SEMS,)),
        "recv_sems": pltpu.SemaphoreType.DMA((RECV_SEMS,)),
        "local_sems": pltpu.SemaphoreType.DMA((17 + 2 * len(CHUNKS),)),
        "shared": {
            "up": pltpu.VMEM((WIDTH, 2 * ROW), BF16),
            "up_t": pltpu.VMEM((2 * ROW, WIDTH), BF16),
            "down": pltpu.VMEM((2 * ROW, WIDTH), BF16),
            "up_total": pltpu.VMEM((WIDTH, 2 * ROW), F32),
            "down_total": pltpu.VMEM((2 * ROW, WIDTH), F32),
        },
        "chunks": [chunk_scratch(size, i) for i, (_, size) in enumerate(CHUNKS)],
    }
    leaves, tree = jax.tree.flatten(scratch)

    def run(*refs):
        kernel(*refs[:7], jax.tree.unflatten(tree, refs[7:]))

    vmem, hbm = pl.BlockSpec(memory_space=pltpu.VMEM), pl.BlockSpec(memory_space=pl.ANY)
    in_grad, up_grad, down_grad = pl.pallas_call(
        run,
        out_shape=(
            pltpu.VMEM((HALF, 640), BF16),
            pltpu.VMEM((WIDTH, 2 * ROW), BF16),
            pltpu.VMEM((2 * ROW, WIDTH), BF16),
        ),
        in_specs=[hbm] * 4,
        out_specs=(vmem, vmem, vmem),
        scratch_shapes=leaves,
        compiler_params=pltpu.CompilerParams(
            collective_id=0, has_side_effects=True, vmem_limit_bytes=59 * 2**20
        ),
        cost_estimate=pl.CostEstimate(
            flops=15_100_000_000, bytes_accessed=10_000_000, transcendentals=245_760
        ),
        name="mlp_backward",
    )(inputs.T, out_grad.T, up_weight, down_weight)
    in_grad, up_grad, down_grad = pl.pallas_call(
        hand_over,
        out_shape=[jax.ShapeDtypeStruct(a.shape, a.dtype) for a in (in_grad, up_grad, down_grad)],
        in_specs=[hbm] * 3,
        out_specs=[hbm] * 3,
        scratch_shapes=[pltpu.SemaphoreType.DMA((3,))],
        compiler_params=pltpu.CompilerParams(vmem_limit_bytes=2**20),
        name="hand_over",
    )(in_grad, up_grad, down_grad)
    return in_grad.T, up_grad, down_grad


def solution(mesh):
    return jax.shard_map(
        body,
        mesh=mesh,
        in_specs=(
            P("gx", ("gy", "gz")),
            P("gx", ("gy", "gz")),
            P("gy", ("gx", "gz")),
            P(("gx", "gz"), "gy"),
        ),
        out_specs=(P("gx", ("gy", "gz")), P("gy", ("gx", "gz")), P(("gx", "gz"), "gy")),
        check_vma=False,
    )
```

```python
import functools

import jax
import jax.numpy as jnp
from jax import lax
from jax.experimental import pallas as pl
from jax.experimental.pallas import tpu as pltpu
from jax.sharding import PartitionSpec as P

gelu_scale = 0.7978845608028654
cubic_term = 0.044715

MESH = pl.DeviceIdType.MESH
BF16, F32 = jnp.bfloat16, jnp.float32

CHUNKS = ((0, 128), (128, 256), (384, 256))
SUMS = (("y", "x"), ("y", "x"), ("y", "x"))
SHARES = (("x", "y"), ("x", "y"), ("y", "y"))
REDUCES = ("z", "z", "direct")
SEND_SEMS = 7 * len(CHUNKS) + 1
RECV_SEMS = 4 + sum(
    19 + sum({"x": 5, "y": 7}[kind] for kind in shares) + {"direct": 1, "z": 3}[reduce]
    for shares, reduce in zip(SHARES, REDUCES)
)
BLOCK = 192
HALF = 96
WIDTH = 768
ROW = 768

PLACES = ((2, 0), (2, 1), (1, 1), (3, 0), (1, 0), (3, 1), (0, 0), (0, 1))


def nn(left, right):
    return jnp.dot(left, right, preferred_element_type=F32)


def nt(left, right):
    return lax.dot_general(left, right, (((1,), (1,)), ((), ())), preferred_element_type=F32)


def aligned(index, step):
    return pl.multiple_of(index * step, step)


class Place:
    def __init__(self):
        self.c = lax.axis_index("gx")
        self.gy = lax.axis_index("gy")
        self.gz = lax.axis_index("gz")
        self.yl, self.x = self.gy // 4, self.gy % 4
        self.yh, self.z = self.gz // 4, self.gz % 4

    def dev(self, dc=0, dyl=0, dx=0, dyh=0, dz=0):
        return (
            (self.c + dc) % 2,
            self.owner((self.yl + dyl) % 2, dx),
            self.zblock(dyh, dz),
        )

    def owner(self, row, dx):
        return row * 4 + (self.x + dx) % 4

    def zblock(self, dyh, dz):
        return ((self.yh + dyh) % 2) * 4 + (self.z + dz) % 4


class Net:
    def __init__(self, send_sems, recv_sems):
        self.send_sems, self.recv_sems = send_sems, recv_sems
        self.outboxes, self.inboxes = 0, 0

    def outbox(self):
        assert self.outboxes < SEND_SEMS
        self.outboxes += 1
        return self.outboxes - 1

    def inbox(self):
        assert self.inboxes < RECV_SEMS
        self.inboxes += 1
        return self.inboxes - 1

    def send(self, src, dst, device, outbox, inbox):
        pltpu.make_async_remote_copy(
            src_ref=src,
            dst_ref=dst,
            send_sem=self.send_sems.at[outbox],
            recv_sem=self.recv_sems.at[inbox],
            device_id=device,
            device_id_type=MESH,
        ).start()

    def arrive(self, inbox, ref):
        pltpu.make_async_copy(ref, ref, self.recv_sems.at[inbox]).wait()

    def leave(self, outbox, ref):
        pltpu.make_async_copy(ref, ref, self.send_sems.at[outbox]).wait()


class Ring:
    def __init__(self, net, here, out, far, near, outbox):
        self.net, self.out, self.far, self.near, self.outbox = net, out, far, near, outbox
        self.far_boxes, self.near_box = (net.inbox(), net.inbox()), net.inbox()
        self.right, self.left = here.dev(dx=1), here.dev(dx=3)

    def push(self, place, dst, device, inbox):
        self.net.send(self.out.at[pl.ds(place * HALF, HALF)], dst, device, self.outbox, inbox)

    def opposite(self):
        self.push(0, self.far.at[0], self.right, self.far_boxes[0])
        self.push(1, self.far.at[1], self.left, self.far_boxes[1])

    def beside(self):
        self.push(2, self.near.at[0, pl.ds(HALF, HALF)], self.right, self.near_box)
        self.push(3, self.near.at[1, pl.ds(0, HALF)], self.left, self.near_box)

    def relay(self, parts):
        for i, device in enumerate((self.right, self.left)):
            part = parts(i)
            self.net.arrive(self.far_boxes[i], self.far.at[i])
            self.out[pl.ds((4 + i) * HALF, HALF)] = (part + self.far[i].astype(F32)).astype(BF16)
            self.push(4 + i, self.near.at[i, pl.ds(i * HALF, HALF)], device, self.near_box)

    def arrive(self):
        self.net.arrive(self.near_box, self.near)

    def add(self, part, half):
        rows = pl.ds(half * HALF, HALF)
        return part + self.near[0, rows].astype(F32) + self.near[1, rows].astype(F32)


class YFirst:
    def __init__(self, net, here, bufs, weight, acts):
        self.net, self.here, self.bufs = net, here, bufs
        self.weight, self.acts = weight, acts
        self.outbox = net.outbox()
        self.ring = Ring(net, here, bufs["out"].at[0], bufs["far"].at[0], bufs["near"].at[0], self.outbox)
        self.y_boxes = [net.inbox() for _ in range(4)]

    def start(self):
        y_out, y_in = self.bufs["y_out"], self.bufs["y_in"]
        for i in range(2):
            rows = pl.ds(i * 2 * BLOCK, 2 * BLOCK)
            y_out[rows] = nn(self.weight[rows], self.acts[...]).astype(BF16)
            for j in (2 * i, 2 * i + 1):
                rows = pl.ds(j * BLOCK, BLOCK)
                self.net.send(y_out.at[rows], y_in.at[rows], self.here.dev(dyl=1), self.outbox, self.y_boxes[j])

    def y_arrive(self, j):
        self.net.arrive(self.y_boxes[j], self.bufs["y_in"].at[pl.ds(j * BLOCK, BLOCK)])

    def rest(self):
        for i in range(2):
            rows, weight_rows = pl.ds(i * 2 * BLOCK, 2 * BLOCK), pl.ds(ROW + i * 2 * BLOCK, 2 * BLOCK)
            self.bufs["held"][rows] = nn(self.weight[weight_rows], self.acts[...])

    def part(self, place):
        rows = pl.ds(place * HALF, HALF)
        return self.bufs["held"][rows] + self.bufs["y_in"][rows].astype(F32)

    def fill(self, i):
        self.y_arrive(i)
        for place in (2 * i, 2 * i + 1):
            self.ring.out[pl.ds(place * HALF, HALF)] = self.part(place).astype(BF16)

    def first(self):
        self.fill(0)
        self.ring.opposite()

    def second(self):
        self.fill(1)
        self.ring.beside()

    def third(self):
        self.y_arrive(2)
        self.ring.relay(lambda i: self.part(4 + i))

    def last(self):
        self.y_arrive(3)
        self.ring.arrive()

    def total(self, half):
        return self.ring.add(self.part(6 + half), half)


class XFirst:
    def __init__(self, net, here, bufs, weight, acts):
        self.net, self.here, self.bufs = net, here, bufs
        self.weight, self.acts = weight, acts
        self.outbox, self.y_box = net.outbox(), net.inbox()
        self.rings = [
            Ring(net, here, bufs["out"].at[i], bufs["far"].at[i], bufs["near"].at[i], self.outbox)
            for i in range(2)
        ]

    def start(self):
        for i, ring in enumerate(self.rings):
            ring.out[pl.ds(0, 2 * BLOCK)] = nn(
                self.weight[pl.ds(i * ROW, 2 * BLOCK)], self.acts[...]
            ).astype(BF16)
            ring.opposite()
        for ring in self.rings:
            ring.beside()

    def rest(self):
        for i in range(2):
            self.bufs["held"][pl.ds(i * 2 * BLOCK, 2 * BLOCK)] = nn(
                self.weight[pl.ds(i * ROW + 2 * BLOCK, 2 * BLOCK)], self.acts[...]
            )

    def part(self, ring, place):
        return self.bufs["held"][pl.ds(ring * 2 * BLOCK + (place - 4) * HALF, HALF)]

    def first(self):
        self.rings[0].relay(lambda i: self.part(0, 4 + i))

    def second(self):
        self.rings[1].relay(lambda i: self.part(1, 4 + i))

    def third(self):
        self.rings[0].arrive()
        y_out, y_in = self.bufs["y_out"].at[pl.ds(0, BLOCK)], self.bufs["y_in"].at[pl.ds(0, BLOCK)]
        for half in range(2):
            y_out[pl.ds(half * HALF, HALF)] = self.rings[0].add(self.part(0, 6 + half), half).astype(BF16)
        self.net.send(y_out, y_in, self.here.dev(dyl=1), self.outbox, self.y_box)

    def last(self):
        self.rings[1].arrive()
        self.net.arrive(self.y_box, self.bufs["y_in"].at[pl.ds(0, BLOCK)])

    def total(self, half):
        rows = pl.ds(half * HALF, HALF)
        return self.rings[1].add(self.part(1, 6 + half), half) + self.bufs["y_in"][rows].astype(F32)


class Share:
    def __init__(self, net, here, buf, row, outbox, apart):
        self.net, self.here, self.buf, self.row, self.outbox = net, here, buf, row, outbox
        self.right, self.left = here.dev(dx=1), here.dev(dx=3)
        self.first_boxes, self.near_box = (net.inbox(), net.inbox()), net.inbox()
        self.far_box = net.inbox() if apart else self.near_box

    def ref(self, dx, half=None):
        owner = self.here.owner(self.row, dx)
        if half is None:
            return self.buf.at[pl.ds(aligned(owner, BLOCK), BLOCK)]
        return self.buf.at[pl.ds(aligned(owner * 2 + half, HALF), HALF)]

    def push(self, ref, device, inbox):
        self.net.send(ref, ref, device, self.outbox, inbox)

    def start(self):
        self.push(self.ref(0, 0), self.right, self.first_boxes[0])
        self.push(self.ref(0, 1), self.left, self.first_boxes[1])
        self.push(self.ref(0, 1), self.right, self.near_box)
        self.push(self.ref(0, 0), self.left, self.near_box)

    def relay(self):
        self.net.arrive(self.first_boxes[0], self.ref(3, 0))
        self.push(self.ref(3, 0), self.right, self.far_box)
        self.net.arrive(self.first_boxes[1], self.ref(1, 1))
        self.push(self.ref(1, 1), self.left, self.far_box)

    def arrive_near(self):
        self.net.arrive(self.near_box, self.ref(1))

    def arrive_far(self):
        self.net.arrive(self.far_box, self.ref(2))

    def arrive_all(self):
        self.net.arrive(self.near_box, self.buf.at[pl.ds(0, 2 * BLOCK)])


class ShareXFirst:
    def __init__(self, net, here, buf):
        self.net, self.here, self.buf = net, here, buf
        self.outbox, self.y_box = net.outbox(), net.inbox()
        self.ring = Share(net, here, buf, here.yl, self.outbox, True)

    def over(self, dx):
        ref = self.ring.ref(dx)
        self.net.send(ref, ref, self.here.dev(dyl=1), self.outbox, self.y_box)

    def start(self):
        self.ring.start()
        self.over(0)

    def first(self):
        self.ring.relay()

    def second(self):
        self.ring.arrive_near()
        self.over(1)
        self.over(3)

    def third(self):
        self.ring.arrive_far()
        self.over(2)

    def own_row(self):
        pass

    def other_row(self):
        self.net.arrive(self.y_box, self.buf.at[pl.ds(aligned(1 - self.here.yl, ROW), ROW)])


class ShareYFirst:
    def __init__(self, net, here, buf):
        self.net, self.here = net, here
        self.outbox, self.y_box = net.outbox(), net.inbox()
        self.rings = [Share(net, here, buf, row, self.outbox, False) for row in (here.yl, 1 - here.yl)]

    def start(self):
        ref = self.rings[0].ref(0)
        self.net.send(ref, ref, self.here.dev(dyl=1), self.outbox, self.y_box)
        self.rings[0].start()

    def first(self):
        self.rings[0].relay()

    def second(self):
        self.net.arrive(self.y_box, self.rings[1].ref(0))
        self.rings[1].start()

    def third(self):
        self.rings[1].relay()

    def own_row(self):
        self.rings[0].arrive_all()

    def other_row(self):
        self.rings[1].arrive_all()


class Gather:
    def __init__(self, net, here, acts, size, first, count, ready, source=None, after=None):
        self.net, self.here, self.size, self.ready = net, here, size, ready
        self.source, self.after = source, after
        self.acts = acts.at[pl.ds(first, count)]
        self.outbox, self.y_box = net.outbox(), net.inbox()
        self.z_boxes, self.core_box = (net.inbox(), net.inbox()), net.inbox()

    def feature_ref(self, zblock):
        rows = pl.ds(aligned(zblock, HALF), HALF)
        return self.acts.at[:, rows, pl.ds(aligned(self.here.c, self.size), self.size)]

    def pass_on(self, zblock, device, inbox, source=None):
        ref = self.feature_ref(zblock)
        if source is None:
            self.net.send(ref, ref, device, self.outbox, inbox)
        else:
            self.net.send(source, ref.at[0], device, self.outbox, inbox)

    def start(self):
        here = self.here
        if self.source is None:
            self.ready()
        self.pass_on(here.gz, here.dev(dyh=1), self.y_box, self.source)
        for dz in (1, 3, 2):
            self.pass_on(here.gz, here.dev(dz=dz), self.z_boxes[0], self.source)
        self.pass_on(here.gz, here.dev(dc=1), self.core_box, self.source)
        if self.after is not None:
            self.after()

    def second(self):
        here = self.here
        block = here.zblock(1, 0)
        self.net.arrive(self.y_box, self.feature_ref(block))
        for dz in (1, 3, 2):
            self.pass_on(block, here.dev(dz=dz), self.z_boxes[1])
        self.pass_on(block, here.dev(dc=1), self.core_box)

    def row(self, dyh):
        here = self.here
        self.net.arrive(self.z_boxes[dyh], self.acts.at[:, pl.ds(0, 3 * HALF), pl.ds(0, self.size)])
        for dz in (3, 1, 2):
            self.pass_on(here.zblock(dyh, dz), here.dev(dc=1), self.core_box)

    def third(self):
        self.row(0)

    def fourth(self):
        self.row(1)

    def last(self):
        theirs = pl.ds(aligned(1 - self.here.c, self.size), self.size)
        self.net.arrive(self.core_box, self.acts.at[:, :, theirs])
        if self.source is not None:
            self.ready()

    def drain(self):
        self.net.leave(self.outbox, self.acts.at[:, pl.ds(0, 15 * HALF // 2)])


class Chunk:
    def __init__(self, index, net, here, bufs, shared):
        self.first, self.size = CHUNKS[index]
        self.index = index
        self.is_first, self.is_last = index == 0, index == len(CHUNKS) - 1
        self.net, self.here, self.bufs, self.shared = net, here, bufs, shared
        sums, shares = {"y": YFirst, "x": XFirst}, {"x": ShareXFirst, "y": ShareYFirst}
        pre, back = (sums[kind] for kind in SUMS[index])
        act, grad = (shares[kind] for kind in SHARES[index])
        acts = bufs["acts"]
        self.pre = pre(net, here, bufs["pre"], shared["up_t"], acts.at[0])
        self.back = back(net, here, bufs["back"], shared["down"], acts.at[1])
        self.act = act(net, here, bufs["activation"])
        self.grad = grad(net, here, bufs["pre_grad"])
        if self.is_first:
            columns = pl.ds(self.first, self.size)
            self.feat = Gather(
                net, here, acts, self.size, 1, 1, lambda: self.loads[1].wait(), shared["out_grad"].at[:, columns]
            )
            self.feat_two = Gather(
                net, here, acts, self.size, 0, 1, lambda: self.loads[0].wait(), shared["inputs"].at[:, columns],
                shared["load_rest"],
            )
        else:
            self.feat = self.feat_two = Gather(net, here, acts, self.size, 0, 2, self.ready)
        self.core_out, self.reduce_out = net.outbox(), net.outbox()
        self.in_grad_box = net.inbox()
        self.reduce_boxes = [net.inbox() for _ in range(1 if REDUCES[index] == "direct" else 3)]

    def ready(self):
        for copy in self.loads:
            copy.wait()

    def load(self):
        here = self.here
        rows = pl.ds(aligned(here.gz, HALF), HALF)
        lanes = pl.ds(aligned(here.c, self.size), self.size)
        self.loads = []
        for i, name in enumerate(("inputs", "out_grad")):
            self.loads.append(
                self.shared["fetch"](
                    self.shared[name].at[:, pl.ds(self.first, self.size)],
                    self.bufs["acts"].at[i, rows, lanes],
                )
            )

    def activate(self):
        self.back.last()
        self.pre.last()
        hidden, back = self.bufs["pre"]["held"], self.bufs["back"]["held"]
        at = 6 * HALF
        for half in range(2):
            rows = pl.ds(at + half * HALF, HALF)
            hidden[rows] = self.pre.total(half)
            back[rows] = self.back.total(half)
        base = self.here.gy * BLOCK

        @pl.loop(0, BLOCK // 16)
        def _(i):
            rows = pl.ds(pl.multiple_of(at + i * 16, 16), 16)
            to = pl.ds(pl.multiple_of(base + i * 16, 16), 16)
            x = hidden[rows, :]
            t = jnp.tanh(gelu_scale * (x + cubic_term * x * x * x))
            deriv = 0.5 * (1.0 + t) + 0.5 * x * (1.0 - t * t) * gelu_scale * (1.0 + 3.0 * cubic_term * x * x)
            self.bufs["activation"][to, :] = (0.5 * x * (1.0 + t)).astype(BF16)
            self.bufs["pre_grad"][to, :] = (back[rows, :] * deriv).astype(BF16)

    def in_grad_rows(self, row, add):
        up, pre_grad, total = self.shared["up"], self.bufs["pre_grad"], self.bufs["in_grad"]
        cols = pl.ds(aligned(row, ROW), ROW)

        @pl.loop(0, 2)
        def _(i):
            rows = pl.ds(pl.multiple_of(i * 384, 384), 384)
            value = nn(up[rows, cols], pre_grad[cols, :])
            total[rows, :] = total[rows, :] + value if add else value

    def put(self, name, rows, cols, value):
        if not self.is_first:
            value = value + self.shared[name + "_total"][rows, cols]
        if self.is_last:
            self.shared[name + "_grad"][rows, cols] = value.astype(BF16)
        else:
            self.shared[name + "_total"][rows, cols] = value

    def up_rows(self, row):
        acts, pre_grad = self.bufs["acts"], self.bufs["pre_grad"]
        cols = pl.ds(aligned(row, ROW), ROW)

        @pl.loop(0, 2)
        def _(i):
            rows = pl.ds(pl.multiple_of(i * 384, 384), 384)
            self.put("up", rows, cols, nt(acts[0, rows, :], pre_grad[cols, :]))

    def down_rows(self, row):
        acts, activation = self.bufs["acts"], self.bufs["activation"]

        @pl.loop(0, 2)
        def _(i):
            rows = pl.ds(pl.multiple_of(row * ROW + i * 384, 384), 384)
            self.put("down", rows, slice(None), nt(activation[rows, :], acts[1]))

    def prepare(self):
        if self.is_first:
            self.shared["turn_up"]()
            self.shared["turn_down"]()

    def in_grad_own(self):
        self.grad.own_row()
        self.in_grad_rows(self.here.yl, False)

    def in_grad_other(self):
        self.grad.other_row()
        self.in_grad_rows(1 - self.here.yl, True)
        self.reduce_start()

    def up_own(self):
        self.up_rows(self.here.yl)

    def up_other(self):
        self.up_rows(1 - self.here.yl)

    def down_own(self):
        self.act.own_row()
        self.down_rows(self.here.yl)

    def down_other(self):
        self.act.other_row()
        self.down_rows(1 - self.here.yl)

    def reduce_start(self):
        theirs = pl.ds(aligned(1 - self.here.c, self.size), self.size)
        self.net.send(
            self.bufs["in_grad"].at[:, theirs], self.bufs["in_grad_core"], self.here.dev(dc=1),
            self.core_out, self.in_grad_box,
        )

    def core_sum(self, zblock):
        rows = pl.ds(aligned(zblock, HALF), HALF)
        mine = pl.ds(aligned(self.here.c, self.size), self.size)
        return self.bufs["in_grad"][rows, mine] + self.bufs["in_grad_core"][rows, :]

    def reduce_send(self, i, value, device, inbox):
        src, dst = self.bufs["in_grad_out"].at[i], self.bufs["in_grad_in"].at[i]
        src[...] = value.astype(BF16)
        self.net.send(src, dst, device, self.reduce_out, inbox)

    def reduce_second(self):
        here = self.here
        self.net.arrive(self.in_grad_box, self.bufs["in_grad_core"])
        if REDUCES[self.index] == "direct":
            offsets = [(dyh, dz) for dyh in (1, 0) for dz in (2, 1, 3, 0)][:-1]
            for i, (dyh, dz) in enumerate(offsets):
                value = self.core_sum(here.zblock(dyh, dz))
                self.reduce_send(i, value, here.dev(dyh=dyh, dz=dz), self.reduce_boxes[0])
            return
        for i, (dyh, dz) in enumerate([(dyh, dz) for dyh in (1, 0) for dz in (2, 1, 3)]):
            value = self.core_sum(here.zblock(dyh, dz))
            self.reduce_send(i, value, here.dev(dz=dz), self.reduce_boxes[1 - dyh])

    def gathered(self, zblock, boxes):
        value = self.core_sum(zblock)
        for box, first, count in boxes:
            self.net.arrive(self.reduce_boxes[box], self.bufs["in_grad_in"].at[pl.ds(first, count)])
            for i in range(first, first + count):
                value = value + self.bufs["in_grad_in"][i].astype(F32)
        return value

    def reduce_third(self):
        if REDUCES[self.index] == "direct":
            return
        value = self.gathered(self.here.zblock(1, 0), ((0, 0, 3),))
        self.reduce_send(6, value, self.here.dev(dyh=1), self.reduce_boxes[2])

    def reduce_last(self):
        boxes = ((0, 0, 7),) if REDUCES[self.index] == "direct" else ((1, 3, 3), (2, 6, 1))
        value = self.gathered(self.here.gz, boxes)
        self.shared["in_grad"][:, pl.ds(self.first, self.size)] = value.astype(BF16)

    def drain(self):
        bufs = self.bufs
        self.feat.drain()
        if self.is_first:
            self.feat_two.drain()
        for part in (self.pre, self.back, self.act, self.grad):
            self.net.leave(part.outbox, bufs["activation"].at[pl.ds(0, 14 * HALF)])
        self.net.leave(self.core_out, bufs["in_grad_core"])
        self.net.leave(self.reduce_out, bufs["in_grad_in"])


def order(chunks):
    a, b, c = chunks
    return (
        a.feat.start, a.feat_two.start, a.feat.second, a.feat_two.second, b.feat.start, a.feat.third, a.prepare,
        a.feat.fourth, a.feat_two.fourth, a.feat_two.third, a.feat.last, b.feat.second, c.feat.start, a.back.start,
        a.feat_two.last, a.pre.start, a.back.rest, b.feat.third, a.back.first, a.pre.rest, a.back.second, a.pre.first,
        b.feat.fourth, c.feat.second, a.pre.second, a.back.third, b.feat.last, b.back.start, b.pre.start,
        c.feat.fourth, b.back.rest, c.feat.third, a.pre.third, b.back.first, b.back.second, a.activate, b.pre.rest,
        a.grad.start, b.pre.second, b.back.third, c.feat.last, c.back.start, c.back.rest, a.grad.first, b.pre.first,
        a.grad.second, a.act.start, c.back.second, c.pre.start, c.pre.rest, a.grad.third, a.in_grad_own, b.pre.third,
        c.pre.second, c.pre.first, a.act.first, a.in_grad_other, b.activate, c.back.first, b.grad.start, a.act.second,
        c.back.third, c.pre.third, b.act.start, b.grad.second, a.reduce_second, b.grad.first, a.act.third, a.down_own,
        a.reduce_third, c.activate, b.grad.third, a.up_own, b.act.first, a.up_other, c.grad.start, b.act.second,
        b.in_grad_own, b.in_grad_other, a.down_other, a.reduce_last, c.grad.second, b.reduce_second, b.up_other,
        c.grad.first, c.grad.third, b.reduce_third, c.act.start, b.up_own, c.in_grad_own, b.reduce_last, b.act.third,
        c.in_grad_other, c.act.first, b.down_own, c.act.second, c.reduce_second, c.reduce_third, c.up_other, c.up_own,
        c.act.third, b.down_other, c.down_own, c.reduce_last, c.down_other,
    )


def chunk_scratch(size, index):
    tokens = 2 * size

    def sums(rows, y_rows):
        return {
            "held": pltpu.VMEM((ROW, tokens), F32),
            "out": pltpu.VMEM((rows, 3 * BLOCK, tokens), BF16),
            "far": pltpu.VMEM((rows, 2, HALF, tokens), BF16),
            "near": pltpu.VMEM((rows, 2, BLOCK, tokens), BF16),
            "y_out": pltpu.VMEM((y_rows, tokens), BF16),
            "y_in": pltpu.VMEM((y_rows, tokens), BF16),
        }

    shapes = {"y": (1, ROW), "x": (2, BLOCK)}
    return {
        "acts": pltpu.VMEM((2, WIDTH, tokens), BF16),
        "pre": sums(*shapes[SUMS[index][0]]),
        "back": sums(*shapes[SUMS[index][1]]),
        "activation": pltpu.VMEM((8 * BLOCK, tokens), BF16),
        "pre_grad": pltpu.VMEM((8 * BLOCK, tokens), BF16),
        "in_grad": pltpu.VMEM((WIDTH, tokens), F32),
        "in_grad_core": pltpu.VMEM((WIDTH, size), F32),
        "in_grad_out": pltpu.VMEM((7, HALF, size), BF16),
        "in_grad_in": pltpu.VMEM((7, HALF, size), BF16),
    }


def kernel(inputs, out_grad, up_hbm, down_hbm, in_grad, up_grad, down_grad, scratch):
    here = Place()
    net = Net(scratch["send_sems"], scratch["recv_sems"])
    shared = dict(scratch["shared"])
    fetched = []

    def fetch(src, dst):
        copy = pltpu.make_async_copy(src, dst, scratch["local_sems"].at[len(fetched)])
        fetched.append(copy)
        copy.start()
        return copy

    shared.update(
        inputs=inputs, out_grad=out_grad, in_grad=in_grad, up_grad=up_grad, down_grad=down_grad, fetch=fetch
    )
    barrier = pltpu.get_barrier_semaphore()
    partners = [here.dev(dc=1), here.dev(dyl=1), here.dev(dx=1), here.dev(dx=3)]
    partners += [here.dev(dyh=dyh, dz=dz) for dyh in range(2) for dz in range(4) if dyh or dz]
    for device in partners:
        pl.semaphore_signal(barrier, inc=1, device_id=device, device_id_type=MESH)

    up_loads, down_loads = [], []

    def load_rest():
        for chunk in chunks:
            chunk.load()
        up_loads.append(fetch(up_hbm, shared["up"]))
        for row in range(2):
            for place, (dx, half) in enumerate(PLACES):
                first = aligned(here.owner((here.yl + 1 - row) % 2, dx) * 2 + half, HALF)
                down_loads.append(
                    fetch(
                        down_hbm.at[pl.ds(first, HALF)],
                        shared["down"].at[pl.ds(row * ROW + place * HALF, HALF)],
                    )
                )

    shared.update(load_rest=load_rest)
    chunks = [Chunk(i, net, here, scratch["chunks"][i], shared) for i in range(len(CHUNKS))]
    natural = down_grad

    def turn_down():
        for copy in down_loads:
            copy.wait()

    def turn_up():
        up_loads[0].wait()
        for i in range(4):
            part = pl.ds(i * 384, 384)
            natural[part, :] = shared["up"][:, part].T
        for row in range(2):
            for place, (dx, half) in enumerate(PLACES):
                source = aligned(here.owner((here.yl + 1 - row) % 2, dx) * 2 + half, HALF)
                shared["up_t"][pl.ds(row * ROW + place * HALF, HALF)] = natural[pl.ds(source, HALF)]

    shared.update(turn_up=turn_up, turn_down=turn_down)
    pl.semaphore_wait(barrier, len(partners))
    for step in order(chunks):
        step()
    for chunk in chunks:
        chunk.drain()


def hand_over(*refs):
    sources, results, sems = refs[:3], refs[3:6], refs[6]
    copies = []
    for i, (source, result) in enumerate(zip(sources, results)):
        copy = pltpu.make_async_copy(source, result, sems.at[i])
        copy.start()
        copies.append(copy)
    for copy in copies:
        copy.wait()


def body(inputs, out_grad, up_weight, down_weight):
    scratch = {
        "send_sems": pltpu.SemaphoreType.DMA((SEND_SEMS,)),
        "recv_sems": pltpu.SemaphoreType.DMA((RECV_SEMS,)),
        "local_sems": pltpu.SemaphoreType.DMA((17 + 2 * len(CHUNKS),)),
        "shared": {
            "up": pltpu.VMEM((WIDTH, 2 * ROW), BF16),
            "up_t": pltpu.VMEM((2 * ROW, WIDTH), BF16),
            "down": pltpu.VMEM((2 * ROW, WIDTH), BF16),
            "up_total": pltpu.VMEM((WIDTH, 2 * ROW), F32),
            "down_total": pltpu.VMEM((2 * ROW, WIDTH), F32),
        },
        "chunks": [chunk_scratch(size, i) for i, (_, size) in enumerate(CHUNKS)],
    }
    leaves, tree = jax.tree.flatten(scratch)

    def run(*refs):
        kernel(*refs[:7], jax.tree.unflatten(tree, refs[7:]))

    vmem, hbm = pl.BlockSpec(memory_space=pltpu.VMEM), pl.BlockSpec(memory_space=pl.ANY)
    in_grad, up_grad, down_grad = pl.pallas_call(
        run,
        out_shape=(
            pltpu.VMEM((HALF, 640), BF16),
            pltpu.VMEM((WIDTH, 2 * ROW), BF16),
            pltpu.VMEM((2 * ROW, WIDTH), BF16),
        ),
        in_specs=[hbm] * 4,
        out_specs=(vmem, vmem, vmem),
        scratch_shapes=leaves,
        compiler_params=pltpu.CompilerParams(
            collective_id=0, has_side_effects=True, vmem_limit_bytes=59 * 2**20
        ),
        cost_estimate=pl.CostEstimate(
            flops=15_100_000_000, bytes_accessed=10_000_000, transcendentals=245_760
        ),
        name="mlp_backward",
    )(inputs.T, out_grad.T, up_weight, down_weight)
    in_grad, up_grad, down_grad = pl.pallas_call(
        hand_over,
        out_shape=[jax.ShapeDtypeStruct(a.shape, a.dtype) for a in (in_grad, up_grad, down_grad)],
        in_specs=[hbm] * 3,
        out_specs=[hbm] * 3,
        scratch_shapes=[pltpu.SemaphoreType.DMA((3,))],
        compiler_params=pltpu.CompilerParams(vmem_limit_bytes=2**20),
        name="hand_over",
    )(in_grad, up_grad, down_grad)
    return in_grad.T, up_grad, down_grad


def solution(mesh):
    return jax.shard_map(
        body,
        mesh=mesh,
        in_specs=(
            P("gx", ("gy", "gz")),
            P("gx", ("gy", "gz")),
            P("gy", ("gx", "gz")),
            P(("gx", "gz"), "gy"),
        ),
        out_specs=(P("gx", ("gy", "gz")), P("gy", ("gx", "gz")), P(("gx", "gz"), "gy")),
        check_vma=False,
    )
```
